32 devices in a mesh: ctx: 16 (over z, y, x), head: 2 (over core).
Axes of the slice: x: 2, y: 2, z: 4, core: 2. Of those that a mesh axis runs over, the one named last changes fastest.
Arguments:
- queries: bfloat16 [4096, 4096], P('ctx', 'head'), may hold values from -12 to 12
- keys: bfloat16 [4096, 4096], P('ctx', 'head'), may hold values from -4 to 4
- values: bfloat16 [4096, 4096], P('ctx', 'head'), may hold values from -6 to 6
- pool_weight: bfloat16 [128, 256], P('ctx'), may hold values from -0.375 to 0.375
- out_weight: bfloat16 [4096, 4096], P('head', 'ctx'), may hold values from -0.09375 to 0.09375
- pattern: int32 [32, 5], replicated, may hold values from 0 to 31, as said below
Outputs:
- mixed: bfloat16 [4096, 4096], P('ctx', 'head')
The draws below stay inside these ranges and needn't reach their ends.
Inputs may be any that keep to these rules, and one draw needn't show every extreme that they name: `pattern`: the flat butterfly with the blocks of each shard relabelled: entry (i, b) names a key block that agrees with block i in all bits above b and differs from it in bit b. For b < 1 the lower bits are arbitrary. For b >= 1 the bits from 1 to b - 1 equal those of i, and over the 2 query blocks of one aligned group of 2 blocks the lowest 1 bits take each of their 2 values once.
All inputs are finite; a program needn't handle non-finite values.
Results may differ from the reference program's by a relative error of at most 0.019.
Values may be sent and summed in bfloat16 or wider, within the bound.
A program may use at most 128 MiB of HBM per device.

```python
import jax
import jax.numpy as jnp
from jax import lax

D = 4096
ATTENTION_HEADS = 32
HEAD_DIMENSION = 128
BLK = 128
LAND = 8
TOK_DEV = 256
BPS = 2
LOCAL_BITS = 1
NBITS = 5
TOKENS = 4096
NBLK = 32
LANDMARK_TOTAL = 128
N_CTX = 16
N_HEAD = 2


def draw_queries(key, part):
    drawn_part = jnp.clip(2.5 * jax.random.normal(jax.random.fold_in(key, 1), (TOKENS, ATTENTION_HEADS * HEAD_DIMENSION)), -12.0, 12.0)
    return drawn_part.astype(jnp.bfloat16)


def draw_keys(key, part):
    drawn_part = jnp.clip(jax.random.normal(jax.random.fold_in(key, 2), (TOKENS, ATTENTION_HEADS * HEAD_DIMENSION)), -4.0, 4.0)
    return drawn_part.astype(jnp.bfloat16)


def draw_pattern(key, part):
    block_index = jnp.arange(NBLK, dtype=jnp.int32)
    group_count = NBLK // BPS
    columns = []
    for level in range(NBITS):
        upper = block_index >> level + 1 << level + 1
        flipped = (block_index >> level & 1 ^ 1) << level
        if level < LOCAL_BITS:
            if level > 0:
                lower = jax.random.randint(jax.random.fold_in(key, level), (NBLK,), 0, 2 ** level).astype(jnp.int32)
            else:
                lower = jnp.zeros((NBLK,), jnp.int32)
            columns.append(upper | flipped | lower)
        else:
            middle = block_index & (1 << level) - BPS
            group_keys = jax.random.split(jax.random.fold_in(key, 100 + level), group_count)
            leaf = jax.vmap(lambda sub_key: jax.random.permutation(sub_key, BPS))(group_keys).reshape(NBLK).astype(jnp.int32)
            columns.append(upper | flipped | middle | leaf)
    return jnp.stack(columns, axis=1).astype(jnp.int32)


def level_of(key, shape, cuts, smallest, top_value):
    loudness = 1.0
    for position, blocks in cuts:
        steps = jax.random.uniform(jax.random.fold_in(jax.random.fold_in(key, 6), position), (blocks,), jnp.float32, smallest / len(cuts), top_value / len(cuts))
        loudness = loudness * jnp.repeat(jnp.exp(steps), shape[position] // blocks).reshape((-1,) + (1,) * (len(shape) - 1 - position))
    return loudness


def scatter_about(stream_key, extent, spread, limit, cuts=(), kind=jnp.bfloat16):
    factor_of = level_of(stream_key, extent, cuts, -0.22, 0.18) if cuts else 1.0
    drawn = jax.random.normal(stream_key, extent, jnp.float32) * spread * factor_of
    return jnp.minimum(jnp.maximum(drawn, -limit), limit).astype(kind)


def setup_inputs(seed: int = 0) -> dict:
    seeds = jax.random.split(jax.random.key(seed), 7)
    return {
        "queries": draw_queries(jax.random.fold_in(seeds[6], 71), 0),
        "keys": draw_keys(jax.random.fold_in(seeds[6], 71), 0),
        "values": scatter_about(seeds[2], (TOKENS, ATTENTION_HEADS * HEAD_DIMENSION), 1.0, 6.0, ((0, 16), (1, 2))),
        "pool_weight": scatter_about(seeds[3], (LANDMARK_TOTAL, TOK_DEV), TOK_DEV ** -0.5, 0.375, ((0, 16),)),
        "out_weight": scatter_about(seeds[4], (ATTENTION_HEADS * HEAD_DIMENSION, D), (ATTENTION_HEADS * HEAD_DIMENSION) ** -0.5, 0.09375, ((0, 2), (1, 16))),
        "pattern": draw_pattern(jax.random.fold_in(seeds[6], 71), 0),
    }


def reference(queries, keys, values, pool_weight, out_weight, pattern):
    col_width = ATTENTION_HEADS * HEAD_DIMENSION
    sharded_keys = keys.reshape(N_CTX, TOK_DEV, col_width).astype(jnp.float32)
    sharded_values = values.reshape(N_CTX, TOK_DEV, col_width).astype(jnp.float32)
    sharded_pooling = pool_weight.reshape(N_CTX, LAND, TOK_DEV).astype(jnp.float32)
    pooled_landmark_keys = jnp.einsum("rmi,riu->rmu", sharded_pooling, sharded_keys).astype(jnp.bfloat16).reshape(LANDMARK_TOTAL, ATTENTION_HEADS, HEAD_DIMENSION)
    pooled_landmark_values = jnp.einsum("rmi,riu->rmu", sharded_pooling, sharded_values).astype(jnp.bfloat16).reshape(LANDMARK_TOTAL, ATTENTION_HEADS, HEAD_DIMENSION)
    key_blocks = keys.reshape(NBLK, BLK, ATTENTION_HEADS, HEAD_DIMENSION)
    value_blocks = values.reshape(NBLK, BLK, ATTENTION_HEADS, HEAD_DIMENSION)
    query_blocks = queries.reshape(NBLK, BLK, ATTENTION_HEADS, HEAD_DIMENSION)
    score_scale = HEAD_DIMENSION ** -0.5

    def one_block(block_index):
        chosen = jnp.concatenate([jnp.reshape(block_index, (1,)).astype(jnp.int32), pattern[block_index].astype(jnp.int32)])
        key_set = jnp.concatenate([key_blocks[chosen].reshape(-1, ATTENTION_HEADS, HEAD_DIMENSION), pooled_landmark_keys], axis=0)
        value_set = jnp.concatenate([value_blocks[chosen].reshape(-1, ATTENTION_HEADS, HEAD_DIMENSION), pooled_landmark_values], axis=0)
        scores = jnp.einsum("qhd,khd->hqk", query_blocks[block_index].astype(jnp.float32), key_set.astype(jnp.float32)) * score_scale
        row_max = jnp.max(scores, axis=-1, keepdims=True)
        weights = jnp.exp(scores - row_max)
        row_sum = jnp.sum(weights, axis=-1)
        rounded = lax.optimization_barrier(weights.astype(jnp.bfloat16))
        summed = jnp.einsum("hqk,khd->qhd", rounded.astype(jnp.float32), value_set.astype(jnp.float32))
        return (summed / row_sum.T[:, :, None]).astype(jnp.bfloat16)

    attended = lax.map(one_block, jnp.arange(NBLK, dtype=jnp.int32))
    group_width = col_width // N_HEAD
    attended = attended.reshape(N_CTX, TOK_DEV, N_HEAD, group_width)
    weight_groups = out_weight.reshape(N_HEAD, group_width, D).astype(jnp.float32)

    def project(shard_rows):
        parts = jnp.einsum("tgc,gcd->gtd", shard_rows.astype(jnp.float32), weight_groups).astype(jnp.bfloat16)
        parts = lax.optimization_barrier(parts)
        return jnp.sum(parts.astype(jnp.float32), axis=0).astype(jnp.bfloat16)

    mixed = lax.map(project, attended)
    return mixed.reshape(TOKENS, D)
```

```python
import functools

import jax
import jax.numpy as jnp
from jax import lax
from jax.experimental import pallas as pl
from jax.experimental.pallas import tpu as pltpu
from jax.sharding import PartitionSpec as P

HEAD_DIMENSION = 128
BLK = 128
NEAR_LEVELS = 1
MESH = pl.DeviceIdType.MESH
PIECES = 2


def flip_bit(index, step):
    return index + step - 2 * step * lax.rem(lax.div(index, step), 2)


def differing_bits(first, second, steps):
    total = 0
    for step in steps:
        a = lax.rem(lax.div(first, step), 2)
        b = lax.rem(lax.div(second, step), 2)
        total = total + step * (a + b - 2 * a * b)
    return total


def scores_of(queries, keys):
    return lax.dot_general(
        queries, keys, (((1,), (1,)), ((), ())), preferred_element_type=jnp.float32
    )


def layer_kernel(n_ctx, n_head, *refs):
    steps = [1 << bit for bit in range(n_ctx.bit_length() - 1)]
    levels = len(steps)
    q_ref, k_ref, v_ref, pool_ref, w_ref, pattern_ref, out_ref = refs[:7]
    refs = refs[7:]
    far_k, refs = refs[:levels], refs[levels:]
    far_v, refs = refs[:levels], refs[levels:]
    (w_buf, marks, acc, top, total, attended, partial, arrived) = refs[:8]
    (kv_send, kv_recv, w_send, w_recv, mark_send, mark_recv, head_send, head_recv, own_sem) = refs[8:]

    tok_rows, col_width = q_ref.shape
    heads = col_width // HEAD_DIMENSION
    blocks = tok_rows // BLK
    land = pool_ref.shape[0]
    depth, w_width = w_ref.shape
    piece_rows = depth // PIECES
    scale = HEAD_DIMENSION ** (-0.5)

    me = lax.axis_index("ctx")
    my_head = lax.axis_index("head")
    partner = {step: flip_bit(me, step) for step in steps}
    head_peer = [lax.rem(my_head + j, n_head) for j in range(n_head)]

    barrier = pltpu.get_barrier_semaphore()
    for step in steps:
        pl.semaphore_signal(barrier, inc=1, device_id={"ctx": partner[step]}, device_id_type=MESH)
    for j in range(1, n_head):
        pl.semaphore_signal(barrier, inc=1, device_id={"head": head_peer[j]}, device_id_type=MESH)
    pl.semaphore_wait(barrier, levels + n_head - 1)

    descending = steps[::-1]
    orders = [descending, descending[:-2] + descending[-2:][::-1]]

    held = [[[0]] for _ in orders]
    for order, stages in zip(orders, held):
        for step in order:
            before = [r for stage in stages for r in stage]
            stages.append([r ^ step for r in before])
    open_sends = []

    def send_w(piece, r, stage):
        step = orders[piece][stage]
        rows = pl.ds(piece * piece_rows, piece_rows)
        source = w_ref.at[rows] if r == 0 else w_buf.at[r, rows]
        copy = pltpu.make_async_remote_copy(
            src_ref=source,
            dst_ref=w_buf.at[r ^ step, rows],
            send_sem=w_send.at[piece, r, stage],
            recv_sem=w_recv.at[piece, r ^ step],
            device_id={"ctx": partner[step]},
            device_id_type=MESH,
        )
        copy.start()
        open_sends.append(copy)

    def wait_w(piece, r):
        rows = pl.ds(piece * piece_rows, piece_rows)
        pltpu.make_async_remote_copy(
            src_ref=w_ref.at[rows],
            dst_ref=w_buf.at[r, rows],
            send_sem=w_send.at[piece, 0, 0],
            recv_sem=w_recv.at[piece, r],
            device_id={"ctx": partner[1]},
            device_id_type=MESH,
        ).wait_recv()

    def forward_w(stage):
        for index in range(len(held[0][stage + 1])):
            for piece in range(PIECES):
                r = held[piece][stage + 1][index]
                wait_w(piece, r)
                for later in range(stage + 1, levels):
                    send_w(piece, r, later)

    kv_copies = {}

    def send_kv(level):
        copies = []
        for which, (source, target) in enumerate(((k_ref, far_k[level]), (v_ref, far_v[level]))):
            copy = pltpu.make_async_remote_copy(
                src_ref=source,
                dst_ref=target,
                send_sem=kv_send.at[level, which],
                recv_sem=kv_recv.at[level, which],
                device_id={"ctx": partner[steps[level]]},
                device_id_type=MESH,
            )
            copy.start()
            copies.append(copy)
        kv_copies[level] = copies

    mark_copies = []

    def send_marks(stage):
        size = 1 << stage
        copy = pltpu.make_async_remote_copy(
            src_ref=marks.at[pl.ds(0, size)],
            dst_ref=marks.at[pl.ds(size, size)],
            send_sem=mark_send.at[stage],
            recv_sem=mark_recv.at[stage],
            device_id={"ctx": partner[size]},
            device_id_type=MESH,
        )
        copy.start()
        mark_copies.append(copy)

    def head_columns(head):
        return pl.ds(pl.multiple_of(head * HEAD_DIMENSION, HEAD_DIMENSION), HEAD_DIMENSION)

    def merge(head, rows, raw, value_set):
        old_top = top[head, rows]
        new_top = jnp.maximum(old_top, jnp.max(raw, axis=-1, keepdims=True))
        weights = jnp.exp((raw - new_top) * scale)
        rescale = jnp.exp((old_top - new_top) * scale)
        total[head, rows] = total[head, rows] * rescale + jnp.sum(weights, axis=-1, keepdims=True)
        acc[head, rows] = acc[head, rows] * rescale + jnp.dot(
            weights.astype(jnp.bfloat16), value_set, preferred_element_type=jnp.float32
        )
        top[head, rows] = new_top

    def near_attention():
        @pl.loop(0, heads)
        def _(head):
            columns = head_columns(head)
            raw = scores_of(q_ref[:, columns], k_ref[:, columns])
            row_top = jnp.max(raw, axis=-1, keepdims=True)
            weights = jnp.exp((raw - row_top) * scale)
            top[head] = row_top
            total[head] = jnp.sum(weights, axis=-1, keepdims=True)
            acc[head] = jnp.dot(
                weights.astype(jnp.bfloat16), v_ref[:, columns], preferred_element_type=jnp.float32
            )

    def mark_attention():
        @pl.loop(0, heads)
        def _(head):
            columns = head_columns(head)
            both = marks[:, :, columns].astype(jnp.float32)
            mark_keys = both[:, :land].reshape(n_ctx * land, HEAD_DIMENSION).astype(jnp.bfloat16)
            mark_values = both[:, land:].reshape(n_ctx * land, HEAD_DIMENSION).astype(jnp.bfloat16)
            merge(head, pl.ds(0, tok_rows), scores_of(q_ref[:, columns], mark_keys), mark_values)

    def chosen(ref, wanted, columns):
        picked = ref[pl.ds(0, BLK), columns]
        for block in range(1, blocks):
            other = ref[pl.ds(block * BLK, BLK), columns]
            picked = lax.select(wanted == block, other, picked)
        return picked

    def far_attention(level):
        first = partner[steps[level]] * blocks
        for copy in kv_copies[level]:
            copy.wait_recv()

        @pl.loop(0, heads)
        def _(head):
            columns = head_columns(head)
            for block in range(blocks):
                wanted = pattern_ref[me * blocks + block, NEAR_LEVELS + level] - first
                rows = pl.ds(block * BLK, BLK)
                far_keys = chosen(far_k[level], wanted, columns)
                far_values = chosen(far_v[level], wanted, columns)
                merge(head, rows, scores_of(q_ref[rows, columns], far_keys), far_values)

    for piece in range(PIECES):
        send_w(piece, 0, 0)
    pooled = [
        jnp.dot(pool_ref[...], ref[...], preferred_element_type=jnp.float32) for ref in (k_ref, v_ref)
    ]
    marks[0] = jnp.concatenate(pooled, axis=0).astype(jnp.bfloat16)
    send_marks(0)
    for level in range(min(2, levels)):
        send_kv(level)
    for stage in range(1, levels):
        for piece in range(PIECES):
            send_w(piece, 0, stage)
    own_copy = pltpu.make_async_copy(w_ref, w_buf.at[0], own_sem.at[0])
    own_copy.start()

    near_attention()
    forward_w(0)
    for level in range(min(2, levels), levels)[::-1]:
        send_kv(level)
    mark_copies[0].wait_recv()
    send_marks(1)
    forward_w(1)
    far_attention(0)
    mark_copies[1].wait_recv()
    for stage in range(2, levels):
        send_marks(stage)
        if stage < levels - 1:
            forward_w(stage)
        far_attention(stage - 1)
        mark_copies[stage].wait_recv()
    mark_attention()
    far_attention(levels - 1)
    forward_w(levels - 1)

    @pl.loop(0, heads)
    def _(head):
        attended[:, head_columns(head)] = (acc[head] / total[head]).astype(jnp.bfloat16)

    own_copy.wait()
    pair = max(1, 128 // w_width)
    share = n_ctx // n_head

    def project(target, row_slot):
        @pl.loop(0, share // pair)
        def _(index):
            parts = []
            for extra in range(pair):
                slot = target * share + index * pair + extra
                r = differing_bits(slot, me, steps)
                parts.append(
                    jnp.dot(attended[...], w_buf[r], preferred_element_type=jnp.float32)
                )
            width = pair * w_width
            whole = parts[0] if pair == 1 else jnp.concatenate(parts, axis=1)
            columns = pl.ds(pl.multiple_of(index * width, width), width)
            partial[row_slot, :, columns] = whole.astype(jnp.bfloat16)

    head_copies = []
    for j in range(1, n_head):
        project(head_peer[j], j)
        copy = pltpu.make_async_remote_copy(
            src_ref=partial.at[j],
            dst_ref=arrived.at[j - 1],
            send_sem=head_send.at[j - 1],
            recv_sem=head_recv.at[j - 1],
            device_id={"head": head_peer[j]},
            device_id_type=MESH,
        )
        copy.start()
        head_copies.append(copy)
    project(my_head, 0)
    for copy in head_copies:
        copy.wait_recv()

    rows_at_once = 32

    @pl.loop(0, tok_rows // rows_at_once)
    def _(index):
        rows = pl.ds(pl.multiple_of(index * rows_at_once, rows_at_once), rows_at_once)
        mixed = partial[0, rows].astype(jnp.float32)
        for j in range(1, n_head):
            mixed += arrived[j - 1, rows].astype(jnp.float32)
        out_ref[rows] = mixed.astype(jnp.bfloat16)

    for copy in open_sends + mark_copies + head_copies:
        copy.wait_send()
    for level in range(levels):
        for copy in kv_copies[level]:
            copy.wait_send()


def on_device(n_ctx, n_head, queries, keys, values, pool_weight, out_weight, pattern):
    tok_rows, col_width = queries.shape
    heads = col_width // HEAD_DIMENSION
    depth, w_width = out_weight.shape
    land = pool_weight.shape[0]
    levels = n_ctx.bit_length() - 1
    share = n_ctx * w_width // n_head
    bf16 = jnp.bfloat16
    in_vmem = pl.BlockSpec(memory_space=pltpu.VMEM)
    return pl.pallas_call(
        functools.partial(layer_kernel, n_ctx, n_head),
        out_shape=jax.ShapeDtypeStruct((tok_rows, share), bf16),
        in_specs=[in_vmem] * 5 + [pl.BlockSpec(memory_space=pltpu.SMEM)],
        out_specs=in_vmem,
        scratch_shapes=[pltpu.VMEM((tok_rows, col_width), bf16)] * (2 * levels)
        + [
            pltpu.VMEM((n_ctx, depth, w_width), bf16),
            pltpu.VMEM((n_ctx, 2 * land, col_width), bf16),
            pltpu.VMEM((heads, tok_rows, HEAD_DIMENSION), jnp.float32),
            pltpu.VMEM((heads, tok_rows, 1), jnp.float32),
            pltpu.VMEM((heads, tok_rows, 1), jnp.float32),
            pltpu.VMEM((tok_rows, col_width), bf16),
            pltpu.VMEM((n_head, tok_rows, share), bf16),
            pltpu.VMEM((n_head - 1, tok_rows, share), bf16),
            pltpu.SemaphoreType.DMA((levels, 2)),
            pltpu.SemaphoreType.DMA((levels, 2)),
            pltpu.SemaphoreType.DMA((PIECES, n_ctx, levels)),
            pltpu.SemaphoreType.DMA((PIECES, n_ctx)),
            pltpu.SemaphoreType.DMA((levels,)),
            pltpu.SemaphoreType.DMA((levels,)),
            pltpu.SemaphoreType.DMA((n_head - 1,)),
            pltpu.SemaphoreType.DMA((n_head - 1,)),
            pltpu.SemaphoreType.DMA((1,)),
        ],
        compiler_params=pltpu.CompilerParams(
            collective_id=0, has_side_effects=True, vmem_limit_bytes=56 * 1024 * 1024
        ),
    )(queries, keys, values, pool_weight, out_weight, pattern)


def solution(mesh):
    in_specs = (
        P("ctx", "head"),
        P("ctx", "head"),
        P("ctx", "head"),
        P("ctx", None),
        P("head", "ctx"),
        P(),
    )
    out_specs = P("ctx", "head")
    body = functools.partial(on_device, mesh.shape["ctx"], mesh.shape["head"])
    return jax.shard_map(
        body, mesh=mesh, in_specs=in_specs, out_specs=out_specs, check_vma=False
    )
```

```python
import functools

import jax
import jax.numpy as jnp
from jax import lax
from jax.experimental import pallas as pl
from jax.experimental.pallas import tpu as pltpu
from jax.sharding import PartitionSpec as P

HEAD_DIMENSION = 128
BLK = 128
NEAR_LEVELS = 1
MESH = pl.DeviceIdType.MESH
PIECES = 2
GROUP = 4


def flip_bit(index, step):
    return index + step - 2 * step * lax.rem(lax.div(index, step), 2)


def differing_bits(first, second, steps):
    total = 0
    for step in steps:
        a = lax.rem(lax.div(first, step), 2)
        b = lax.rem(lax.div(second, step), 2)
        total = total + step * (a + b - 2 * a * b)
    return total


def scores_of(queries, keys):
    return lax.dot_general(
        queries, keys, (((1,), (1,)), ((), ())), preferred_element_type=jnp.float32
    )


def layer_kernel(n_ctx, n_head, *refs):
    steps = [1 << bit for bit in range(n_ctx.bit_length() - 1)]
    levels = len(steps)
    q_ref, k_ref, v_ref, pool_ref, w_ref, pattern_ref, out_ref = refs[:7]
    refs = refs[7:]
    far_k, refs = refs[:levels], refs[levels:]
    far_v, refs = refs[:levels], refs[levels:]
    (w_buf, marks, acc, top, total, attended, partial, arrived, summed, shared) = refs[:10]
    (kv_send, kv_recv, w_send, w_recv, mark_send, mark_recv) = refs[10:16]
    (att_send, att_recv, head_send, head_recv, out_send, out_recv) = refs[16:]

    tok_rows, col_width = q_ref.shape
    heads = col_width // HEAD_DIMENSION
    blocks = tok_rows // BLK
    land = pool_ref.shape[0]
    depth, w_width = w_ref.shape
    piece_rows = depth // PIECES
    scale = HEAD_DIMENSION ** (-0.5)

    me = lax.axis_index("ctx")
    my_head = lax.axis_index("head")
    partner = {step: flip_bit(me, step) for step in steps}
    head_peer = [lax.rem(my_head + j, n_head) for j in range(n_head)]

    barrier = pltpu.get_barrier_semaphore()
    for step in steps:
        pl.semaphore_signal(barrier, inc=1, device_id={"ctx": partner[step]}, device_id_type=MESH)
    across = flip_bit(partner[1], 2)
    member = [me, partner[1], partner[2], across]
    pl.semaphore_signal(barrier, inc=1, device_id={"ctx": across}, device_id_type=MESH)
    for j in range(1, n_head):
        pl.semaphore_signal(barrier, inc=1, device_id={"head": head_peer[j]}, device_id_type=MESH)
    pl.semaphore_wait(barrier, levels + n_head)

    order = steps[2:][::-1]
    held = [[0]]
    for step in order:
        before = [r for stage in held for r in stage]
        held.append([r ^ step for r in before])
    open_sends = []

    def send_w(piece, r, stage):
        step = order[stage]
        rows = pl.ds(piece * piece_rows, piece_rows)
        source = w_ref.at[rows] if r == 0 else w_buf.at[r // GROUP, rows]
        copy = pltpu.make_async_remote_copy(
            src_ref=source,
            dst_ref=w_buf.at[(r ^ step) // GROUP, rows],
            send_sem=w_send.at[piece, r // GROUP, stage],
            recv_sem=w_recv.at[piece, (r ^ step) // GROUP],
            device_id={"ctx": partner[step]},
            device_id_type=MESH,
        )
        copy.start()
        open_sends.append(copy)

    def wait_w(piece, r):
        rows = pl.ds(piece * piece_rows, piece_rows)
        pltpu.make_async_remote_copy(
            src_ref=w_ref.at[rows],
            dst_ref=w_buf.at[r // GROUP, rows],
            send_sem=w_send.at[piece, 0, 0],
            recv_sem=w_recv.at[piece, r // GROUP],
            device_id={"ctx": partner[1]},
            device_id_type=MESH,
        ).wait_recv()

    def forward_w(stage):
        for r in held[stage + 1]:
            for piece in range(PIECES):
                wait_w(piece, r)
                for later in range(stage + 1, len(order)):
                    send_w(piece, r, later)

    kv_copies = {}

    def send_kv(level, which):
        source, target = ((k_ref, far_k[level]), (v_ref, far_v[level]))[which]
        copy = pltpu.make_async_remote_copy(
            src_ref=source,
            dst_ref=target,
            send_sem=kv_send.at[level, which],
            recv_sem=kv_recv.at[level, which],
            device_id={"ctx": partner[steps[level]]},
            device_id_type=MESH,
        )
        copy.start()
        kv_copies[level, which] = copy

    mark_copies = []

    def send_marks(stage):
        size = 1 << stage
        copy = pltpu.make_async_remote_copy(
            src_ref=marks.at[pl.ds(0, size)],
            dst_ref=marks.at[pl.ds(size, size)],
            send_sem=mark_send.at[stage],
            recv_sem=mark_recv.at[stage],
            device_id={"ctx": partner[steps[levels - 1 - stage]]},
            device_id_type=MESH,
        )
        copy.start()
        mark_copies.append(copy)

    def head_columns(head):
        return pl.ds(pl.multiple_of(head * HEAD_DIMENSION, HEAD_DIMENSION), HEAD_DIMENSION)

    def merge(head, rows, raw, value_set):
        old_top = top[head, rows]
        new_top = jnp.maximum(old_top, jnp.max(raw, axis=-1, keepdims=True))
        weights = jnp.exp((raw - new_top) * scale)
        rescale = jnp.exp((old_top - new_top) * scale)
        total[head, rows] = total[head, rows] * rescale + jnp.sum(weights, axis=-1, keepdims=True)
        acc[head, rows] = acc[head, rows] * rescale + jnp.dot(
            weights.astype(jnp.bfloat16), value_set, preferred_element_type=jnp.float32
        )
        top[head, rows] = new_top

    def near_attention():
        @pl.loop(0, heads)
        def _(head):
            columns = head_columns(head)
            raw = scores_of(q_ref[:, columns], k_ref[:, columns])
            row_top = jnp.max(raw, axis=-1, keepdims=True)
            weights = jnp.exp((raw - row_top) * scale)
            top[head] = row_top
            total[head] = jnp.sum(weights, axis=-1, keepdims=True)
            acc[head] = jnp.dot(
                weights.astype(jnp.bfloat16), v_ref[:, columns], preferred_element_type=jnp.float32
            )

    def mark_attention():
        @pl.loop(0, heads)
        def _(head):
            columns = head_columns(head)
            both = marks[:, :, columns].astype(jnp.float32)
            mark_keys = both[:, :land].reshape(n_ctx * land, HEAD_DIMENSION).astype(jnp.bfloat16)
            mark_values = both[:, land:].reshape(n_ctx * land, HEAD_DIMENSION).astype(jnp.bfloat16)
            merge(head, pl.ds(0, tok_rows), scores_of(q_ref[:, columns], mark_keys), mark_values)

    def chosen(ref, wanted, columns):
        picked = ref[pl.ds(0, BLK), columns]
        for block in range(1, blocks):
            other = ref[pl.ds(block * BLK, BLK), columns]
            picked = lax.select(wanted == block, other, picked)
        return picked

    def far_attention(level):
        first = partner[steps[level]] * blocks
        for which in range(2):
            if (level, which) != (levels - 1, 0):
                kv_copies[level, which].wait_recv()

        @pl.loop(0, heads)
        def _(head):
            columns = head_columns(head)
            for block in range(blocks):
                wanted = pattern_ref[me * blocks + block, NEAR_LEVELS + level] - first
                rows = pl.ds(block * BLK, BLK)
                far_keys = chosen(far_k[level], wanted, columns)
                far_values = chosen(far_v[level], wanted, columns)
                merge(head, rows, scores_of(q_ref[rows, columns], far_keys), far_values)

    half = col_width // 2
    att_copies = {}

    def send_attended(source, piece, step):
        columns = pl.ds(piece * half, half)
        copy = pltpu.make_async_remote_copy(
            src_ref=attended.at[source, :, columns],
            dst_ref=attended.at[source ^ step, :, columns],
            send_sem=att_send.at[source ^ step, piece],
            recv_sem=att_recv.at[source ^ step, piece],
            device_id={"ctx": partner[step]},
            device_id_type=MESH,
        )
        copy.start()
        att_copies[source ^ step, piece] = copy

    pooled = [
        jnp.dot(pool_ref[...], ref[...], preferred_element_type=jnp.float32) for ref in (k_ref, v_ref)
    ]
    marks[0] = jnp.concatenate(pooled, axis=0).astype(jnp.bfloat16)
    send_marks(0)
    for which in range(2):
        for level in range(levels)[::-1]:
            send_kv(level, which)

    near_attention()
    mark_copies[0].wait_recv()
    send_marks(1)
    far_attention(0)
    far_attention(1)
    kv_copies[levels - 1, 0].wait_recv()
    for stage in range(len(order)):
        for piece in range(PIECES):
            send_w(piece, 0, stage)
    for stage in range(2, levels):
        mark_copies[stage - 1].wait_recv()
        send_marks(stage)
        far_attention(levels + 1 - stage)
    mark_copies[levels - 1].wait_recv()
    mark_attention()

    @pl.loop(0, heads)
    def _(head):
        attended[0, :, head_columns(head)] = (acc[head] / total[head]).astype(jnp.bfloat16)

    for piece in range(2):
        for step in (1 << piece, 2 >> piece):
            send_attended(0, piece, step)
    for piece in range(2):
        att_copies[1 << piece, piece].wait_recv()
        send_attended(1 << piece, piece, 2 >> piece)
    for stage in range(len(order) - 1):
        forward_w(stage)
    for piece in range(2):
        att_copies[2 >> piece, piece].wait_recv()
        att_copies[3, piece].wait_recv()

    turns = n_ctx // GROUP
    share = turns // n_head

    def project(r):
        turn = lax.div(differing_bits(me, r, steps), GROUP)

        @pl.loop(0, GROUP)
        def _(index):
            columns = w_ref[...] if r == 0 else w_buf[r // GROUP]
            rows = jnp.dot(attended[index], columns, preferred_element_type=jnp.float32)
            partial[index, turn] = rows.astype(jnp.bfloat16)

    for stage in range(len(order)):
        for r in held[stage]:
            project(r)
    for r in held[len(order)]:
        for piece in range(PIECES):
            wait_w(piece, r)
        project(r)

    head_copies = {}
    for index in range(GROUP)[::-1]:
        for j in range(1, n_head):
            copy = pltpu.make_async_remote_copy(
                src_ref=partial.at[index, pl.ds(head_peer[j] * share, share)],
                dst_ref=arrived.at[j - 1, index],
                send_sem=head_send.at[j - 1, index],
                recv_sem=head_recv.at[j - 1, index],
                device_id={"head": head_peer[j]},
                device_id_type=MESH,
            )
            copy.start()
            head_copies[index, j] = copy
    out_copies = []
    for index in range(GROUP)[::-1]:
        for j in range(1, n_head):
            head_copies[index, j].wait_recv()
        target = summed if index else shared
        for turn in range(share):
            mixed = partial[index, my_head * share + turn].astype(jnp.float32)
            for j in range(1, n_head):
                mixed += arrived[j - 1, index, turn].astype(jnp.float32)
            target[index, turn] = mixed.astype(jnp.bfloat16)
        if index:
            copy = pltpu.make_async_remote_copy(
                src_ref=summed.at[index],
                dst_ref=shared.at[index],
                send_sem=out_send.at[index],
                recv_sem=out_recv.at[index],
                device_id={"ctx": member[index]},
                device_id_type=MESH,
            )
            copy.start()
            out_copies.append(copy)
    for copy in out_copies:
        copy.wait_recv()

    pair = max(1, 128 // w_width)
    for first in range(0, share * GROUP, pair):
        parts = []
        for slot in range(first, first + pair):
            index = differing_bits(lax.rem(me, GROUP), slot % GROUP, (1, 2))
            parts.append(shared[index, slot // GROUP])
        whole = parts[0] if pair == 1 else jnp.concatenate(parts, axis=1)
        out_ref[:, pl.ds(first * w_width, pair * w_width)] = whole

    sent = open_sends + mark_copies + out_copies
    for copies in (kv_copies, att_copies, head_copies):
        sent.extend(copies.values())
    for copy in sent:
        copy.wait_send()


def on_device(n_ctx, n_head, queries, keys, values, pool_weight, out_weight, pattern):
    tok_rows, col_width = queries.shape
    heads = col_width // HEAD_DIMENSION
    depth, w_width = out_weight.shape
    land = pool_weight.shape[0]
    levels = n_ctx.bit_length() - 1
    turns = n_ctx // GROUP
    share = turns // n_head
    bf16 = jnp.bfloat16
    in_vmem = pl.BlockSpec(memory_space=pltpu.VMEM)
    return pl.pallas_call(
        functools.partial(layer_kernel, n_ctx, n_head),
        out_shape=jax.ShapeDtypeStruct((tok_rows, share * GROUP * w_width), bf16),
        in_specs=[in_vmem] * 5 + [pl.BlockSpec(memory_space=pltpu.SMEM)],
        out_specs=in_vmem,
        scratch_shapes=[pltpu.VMEM((tok_rows, col_width), bf16)] * (2 * levels)
        + [
            pltpu.VMEM((turns, depth, w_width), bf16),
            pltpu.VMEM((n_ctx, 2 * land, col_width), bf16),
            pltpu.VMEM((heads, tok_rows, HEAD_DIMENSION), jnp.float32),
            pltpu.VMEM((heads, tok_rows, 1), jnp.float32),
            pltpu.VMEM((heads, tok_rows, 1), jnp.float32),
            pltpu.VMEM((GROUP, tok_rows, col_width), bf16),
            pltpu.VMEM((GROUP, turns, tok_rows, w_width), bf16),
            pltpu.VMEM((n_head - 1, GROUP, share, tok_rows, w_width), bf16),
            pltpu.VMEM((GROUP, share, tok_rows, w_width), bf16),
            pltpu.VMEM((GROUP, share, tok_rows, w_width), bf16),
            pltpu.SemaphoreType.DMA((levels, 2)),
            pltpu.SemaphoreType.DMA((levels, 2)),
            pltpu.SemaphoreType.DMA((PIECES, turns, levels)),
            pltpu.SemaphoreType.DMA((PIECES, turns)),
            pltpu.SemaphoreType.DMA((levels,)),
            pltpu.SemaphoreType.DMA((levels,)),
            pltpu.SemaphoreType.DMA((GROUP, 2)),
            pltpu.SemaphoreType.DMA((GROUP, 2)),
            pltpu.SemaphoreType.DMA((n_head - 1, GROUP)),
            pltpu.SemaphoreType.DMA((n_head - 1, GROUP)),
            pltpu.SemaphoreType.DMA((GROUP,)),
            pltpu.SemaphoreType.DMA((GROUP,)),
        ],
        compiler_params=pltpu.CompilerParams(
            collective_id=0, has_side_effects=True, vmem_limit_bytes=56 * 1024 * 1024
        ),
    )(queries, keys, values, pool_weight, out_weight, pattern)


def solution(mesh):
    in_specs = (
        P("ctx", "head"),
        P("ctx", "head"),
        P("ctx", "head"),
        P("ctx", None),
        P("head", "ctx"),
        P(),
    )
    out_specs = P("ctx", "head")
    body = functools.partial(on_device, mesh.shape["ctx"], mesh.shape["head"])
    return jax.shard_map(
        body, mesh=mesh, in_specs=in_specs, out_specs=out_specs, check_vma=False
    )
```

```python
import functools

import jax
import jax.numpy as jnp
from jax import lax
from jax.experimental import pallas as pl
from jax.experimental.pallas import tpu as pltpu
from jax.sharding import PartitionSpec as P

HEAD_DIMENSION = 128
BLK = 128
NEAR_LEVELS = 1
MESH = pl.DeviceIdType.MESH
PIECES = 4
GROUP = 4


def flip_bit(index, step):
    return index + step - 2 * step * lax.rem(lax.div(index, step), 2)


def differing_bits(first, second, steps):
    total = 0
    for step in steps:
        a = lax.rem(lax.div(first, step), 2)
        b = lax.rem(lax.div(second, step), 2)
        total = total + step * (a + b - 2 * a * b)
    return total


def scores_of(queries, keys):
    return lax.dot_general(
        queries, keys, (((1,), (1,)), ((), ())), preferred_element_type=jnp.float32
    )


def layer_kernel(n_ctx, n_head, *refs):
    steps = [1 << bit for bit in range(n_ctx.bit_length() - 1)]
    levels = len(steps)
    q_ref, k_ref, v_ref, pool_ref, w_ref, pattern_ref, out_ref = refs[:7]
    refs = refs[7:]
    far_k, refs = refs[:levels], refs[levels:]
    far_v, refs = refs[:levels], refs[levels:]
    (w_buf, marks, acc, top, total, attended, partial, arrived, summed, shared) = refs[:10]
    (kv_send, kv_recv, w_send, w_recv, mark_send, mark_recv) = refs[10:16]
    (att_send, att_recv, head_send, head_recv, out_send, out_recv) = refs[16:]

    tok_rows, col_width = q_ref.shape
    heads = col_width // HEAD_DIMENSION
    blocks = tok_rows // BLK
    land = pool_ref.shape[0]
    depth, w_width = w_ref.shape
    piece_rows = depth // PIECES
    scale = HEAD_DIMENSION ** (-0.5)

    me = lax.axis_index("ctx")
    my_head = lax.axis_index("head")
    partner = {step: flip_bit(me, step) for step in steps}
    head_peer = [lax.rem(my_head + j, n_head) for j in range(n_head)]

    barrier = pltpu.get_barrier_semaphore()
    for step in steps:
        pl.semaphore_signal(barrier, inc=1, device_id={"ctx": partner[step]}, device_id_type=MESH)
    across = flip_bit(partner[1], 2)
    member = [me, partner[1], partner[2], across]
    pl.semaphore_signal(barrier, inc=1, device_id={"ctx": across}, device_id_type=MESH)
    for j in range(1, n_head):
        pl.semaphore_signal(barrier, inc=1, device_id={"head": head_peer[j]}, device_id_type=MESH)
    pl.semaphore_wait(barrier, levels + n_head)

    order = steps[2:][::-1]
    held = [[0]]
    for step in order:
        before = [r for stage in held for r in stage]
        held.append([r ^ step for r in before])
    open_sends = []

    def send_w(piece, r, stage):
        step = order[stage]
        rows = pl.ds(piece * piece_rows, piece_rows)
        source = w_ref.at[rows] if r == 0 else w_buf.at[r // GROUP, rows]
        copy = pltpu.make_async_remote_copy(
            src_ref=source,
            dst_ref=w_buf.at[(r ^ step) // GROUP, rows],
            send_sem=w_send.at[piece, r // GROUP, stage],
            recv_sem=w_recv.at[piece, (r ^ step) // GROUP],
            device_id={"ctx": partner[step]},
            device_id_type=MESH,
        )
        copy.start()
        open_sends.append(copy)

    def wait_w(piece, r):
        rows = pl.ds(piece * piece_rows, piece_rows)
        pltpu.make_async_remote_copy(
            src_ref=w_ref.at[rows],
            dst_ref=w_buf.at[r // GROUP, rows],
            send_sem=w_send.at[piece, 0, 0],
            recv_sem=w_recv.at[piece, r // GROUP],
            device_id={"ctx": partner[1]},
            device_id_type=MESH,
        ).wait_recv()

    def forward_w(stage):
        for r in held[stage + 1]:
            for piece in range(PIECES):
                wait_w(piece, r)
                for later in range(stage + 1, len(order)):
                    send_w(piece, r, later)

    kv_copies = {}

    def send_kv(level, which):
        source, target = ((k_ref, far_k[level]), (v_ref, far_v[level]))[which]
        copy = pltpu.make_async_remote_copy(
            src_ref=source,
            dst_ref=target,
            send_sem=kv_send.at[level, which],
            recv_sem=kv_recv.at[level, which],
            device_id={"ctx": partner[steps[level]]},
            device_id_type=MESH,
        )
        copy.start()
        kv_copies[level, which] = copy

    mark_copies = []

    def send_marks(stage):
        size = 1 << stage
        copy = pltpu.make_async_remote_copy(
            src_ref=marks.at[pl.ds(0, size)],
            dst_ref=marks.at[pl.ds(size, size)],
            send_sem=mark_send.at[stage],
            recv_sem=mark_recv.at[stage],
            device_id={"ctx": partner[steps[levels - 1 - stage]]},
            device_id_type=MESH,
        )
        copy.start()
        mark_copies.append(copy)

    def head_columns(head):
        return pl.ds(pl.multiple_of(head * HEAD_DIMENSION, HEAD_DIMENSION), HEAD_DIMENSION)

    def merge(entries):
        merged = []
        for head, rows, raw, value_set in entries:
            old_top = top[head, rows]
            new_top = jnp.maximum(old_top, jnp.max(raw, axis=-1, keepdims=True))
            weights = jnp.exp((raw - new_top) * scale)
            rescale = jnp.exp((old_top - new_top) * scale)
            new_total = total[head, rows] * rescale + jnp.sum(weights, axis=-1, keepdims=True)
            new_acc = acc[head, rows] * rescale + jnp.dot(
                weights.astype(jnp.bfloat16), value_set, preferred_element_type=jnp.float32
            )
            merged.append((new_top, new_total, new_acc))
        for (head, rows, _, _), (new_top, new_total, new_acc) in zip(entries, merged):
            top[head, rows] = new_top
            total[head, rows] = new_total
            acc[head, rows] = new_acc

    def near_attention():
        @pl.loop(0, heads // 2)
        def _(index):
            found = []
            for head in (index * 2, index * 2 + 1):
                columns = head_columns(head)
                raw = scores_of(q_ref[:, columns], k_ref[:, columns])
                row_top = jnp.max(raw, axis=-1, keepdims=True)
                weights = jnp.exp((raw - row_top) * scale)
                row_sum = jnp.sum(weights, axis=-1, keepdims=True)
                weighted = jnp.dot(
                    weights.astype(jnp.bfloat16),
                    v_ref[:, columns],
                    preferred_element_type=jnp.float32,
                )
                found.append((head, row_top, row_sum, weighted))
            for head, row_top, row_sum, weighted in found:
                top[head] = row_top
                total[head] = row_sum
                acc[head] = weighted

    def mark_attention():
        @pl.loop(0, heads // 2)
        def _(index):
            entries = []
            for head in (index * 2, index * 2 + 1):
                columns = head_columns(head)
                both = marks[:, :, columns].astype(jnp.float32)
                flat = (n_ctx * land, HEAD_DIMENSION)
                mark_keys = both[:, :land].reshape(flat).astype(jnp.bfloat16)
                mark_values = both[:, land:].reshape(flat).astype(jnp.bfloat16)
                raw = scores_of(q_ref[:, columns], mark_keys)
                entries.append((head, pl.ds(0, tok_rows), raw, mark_values))
            merge(entries)

    def chosen(ref, wanted, columns):
        picked = ref[pl.ds(0, BLK), columns]
        for block in range(1, blocks):
            other = ref[pl.ds(block * BLK, BLK), columns]
            picked = lax.select(wanted == block, other, picked)
        return picked

    def far_attention(level):
        first = partner[steps[level]] * blocks
        for which in range(2):
            if (level, which) != (levels - 1, 0):
                kv_copies[level, which].wait_recv()

        @pl.loop(0, heads // 4)
        def _(index):
            entries = []
            for extra in range(4):
                head = index * 4 + extra
                columns = head_columns(head)
                for block in range(blocks):
                    wanted = pattern_ref[me * blocks + block, NEAR_LEVELS + level] - first
                    rows = pl.ds(block * BLK, BLK)
                    far_keys = chosen(far_k[level], wanted, columns)
                    far_values = chosen(far_v[level], wanted, columns)
                    raw = scores_of(q_ref[rows, columns], far_keys)
                    entries.append((head, rows, raw, far_values))
            merge(entries)

    half = col_width // 2
    att_copies = {}

    def send_attended(source, piece, step):
        columns = pl.ds(piece * half, half)
        copy = pltpu.make_async_remote_copy(
            src_ref=attended.at[source, :, columns],
            dst_ref=attended.at[source ^ step, :, columns],
            send_sem=att_send.at[source ^ step, piece],
            recv_sem=att_recv.at[source ^ step, piece],
            device_id={"ctx": partner[step]},
            device_id_type=MESH,
        )
        copy.start()
        att_copies[source ^ step, piece] = copy

    pooled = [
        jnp.dot(pool_ref[...], ref[...], preferred_element_type=jnp.float32) for ref in (k_ref, v_ref)
    ]
    marks[0] = jnp.concatenate(pooled, axis=0).astype(jnp.bfloat16)
    send_marks(0)
    for which in range(2):
        for level in range(levels)[::-1]:
            send_kv(level, which)

    near_attention()
    mark_copies[0].wait_recv()
    send_marks(1)
    far_attention(0)
    far_attention(1)
    kv_copies[levels - 1, 0].wait_recv()
    for stage in range(len(order)):
        for piece in range(PIECES):
            send_w(piece, 0, stage)
    for stage in range(2, levels):
        mark_copies[stage - 1].wait_recv()
        send_marks(stage)
        far_attention(levels + 1 - stage)
    mark_copies[levels - 1].wait_recv()
    mark_attention()

    @pl.loop(0, heads)
    def _(head):
        attended[0, :, head_columns(head)] = (acc[head] / total[head]).astype(jnp.bfloat16)

    for piece in range(2):
        for step in (1 << piece, 2 >> piece):
            send_attended(0, piece, step)
    for piece in range(2):
        att_copies[1 << piece, piece].wait_recv()
        send_attended(1 << piece, piece, 2 >> piece)
    for stage in range(len(order) - 1):
        forward_w(stage)
    for piece in range(2):
        att_copies[2 >> piece, piece].wait_recv()
        att_copies[3, piece].wait_recv()

    turns = n_ctx // GROUP
    share = turns // n_head

    def project(r):
        turn = lax.div(differing_bits(me, r, steps), GROUP)

        @pl.loop(0, GROUP)
        def _(index):
            columns = w_ref[...] if r == 0 else w_buf[r // GROUP]
            rows = jnp.dot(attended[index], columns, preferred_element_type=jnp.float32)
            partial[index, turn] = rows.astype(jnp.bfloat16)

    my_turn = lax.div(me, GROUP)
    bits = [1 << bit for bit in range(turns.bit_length() - 1)]
    low_bits = [bit for bit in bits if bit < share]
    head_copies = {}
    out_copies = []

    def send_partials(low, turn):
        for index in range(GROUP)[::-1]:
            for j in range(1, n_head):
                copy = pltpu.make_async_remote_copy(
                    src_ref=partial.at[index, head_peer[j] * share + turn],
                    dst_ref=arrived.at[j - 1, index, turn],
                    send_sem=head_send.at[j - 1, index, low],
                    recv_sem=head_recv.at[j - 1, index, low],
                    device_id={"head": head_peer[j]},
                    device_id_type=MESH,
                )
                copy.start()
                head_copies[index, j, low] = copy

    def send_sums(low, turn):
        for index in range(GROUP)[::-1]:
            mixed = partial[index, my_head * share + turn].astype(jnp.float32)
            for j in range(1, n_head):
                head_copies[index, j, low].wait_recv()
                mixed += arrived[j - 1, index, turn].astype(jnp.float32)
            target = summed if index else shared
            target[index, turn] = mixed.astype(jnp.bfloat16)
            if index:
                copy = pltpu.make_async_remote_copy(
                    src_ref=summed.at[index, turn],
                    dst_ref=shared.at[index, turn],
                    send_sem=out_send.at[index, low],
                    recv_sem=out_recv.at[index, low],
                    device_id={"ctx": member[index]},
                    device_id_type=MESH,
                )
                copy.start()
                out_copies.append(copy)

    late = set(held[len(order)])
    everything = [r for stage in held for r in stage]
    for low in range(share):
        turn = differing_bits(lax.rem(my_turn, share), low, low_bits)
        for r in everything:
            if (r // GROUP) % share == low:
                if r in late:
                    for piece in range(PIECES):
                        wait_w(piece, r)
                project(r)
        send_partials(low, turn)
        send_sums(low, turn)
    for copy in out_copies:
        copy.wait_recv()

    pair = max(1, 128 // w_width)
    for first in range(0, share * GROUP, pair):
        parts = []
        for slot in range(first, first + pair):
            index = differing_bits(lax.rem(me, GROUP), slot % GROUP, (1, 2))
            parts.append(shared[index, slot // GROUP])
        whole = parts[0] if pair == 1 else jnp.concatenate(parts, axis=1)
        out_ref[:, pl.ds(first * w_width, pair * w_width)] = whole

    sent = open_sends + mark_copies + out_copies
    for copies in (kv_copies, att_copies, head_copies):
        sent.extend(copies.values())
    for copy in sent:
        copy.wait_send()


def on_device(n_ctx, n_head, queries, keys, values, pool_weight, out_weight, pattern):
    tok_rows, col_width = queries.shape
    heads = col_width // HEAD_DIMENSION
    depth, w_width = out_weight.shape
    land = pool_weight.shape[0]
    levels = n_ctx.bit_length() - 1
    turns = n_ctx // GROUP
    share = turns // n_head
    bf16 = jnp.bfloat16
    in_vmem = pl.BlockSpec(memory_space=pltpu.VMEM)
    return pl.pallas_call(
        functools.partial(layer_kernel, n_ctx, n_head),
        out_shape=jax.ShapeDtypeStruct((tok_rows, share * GROUP * w_width), bf16),
        in_specs=[in_vmem] * 5 + [pl.BlockSpec(memory_space=pltpu.SMEM)],
        out_specs=in_vmem,
        scratch_shapes=[pltpu.VMEM((tok_rows, col_width), bf16)] * (2 * levels)
        + [
            pltpu.VMEM((turns, depth, w_width), bf16),
            pltpu.VMEM((n_ctx, 2 * land, col_width), bf16),
            pltpu.VMEM((heads, tok_rows, HEAD_DIMENSION), jnp.float32),
            pltpu.VMEM((heads, tok_rows, 1), jnp.float32),
            pltpu.VMEM((heads, tok_rows, 1), jnp.float32),
            pltpu.VMEM((GROUP, tok_rows, col_width), bf16),
            pltpu.VMEM((GROUP, turns, tok_rows, w_width), bf16),
            pltpu.VMEM((n_head - 1, GROUP, share, tok_rows, w_width), bf16),
            pltpu.VMEM((GROUP, share, tok_rows, w_width), bf16),
            pltpu.VMEM((GROUP, share, tok_rows, w_width), bf16),
            pltpu.SemaphoreType.DMA((levels, 2)),
            pltpu.SemaphoreType.DMA((levels, 2)),
            pltpu.SemaphoreType.DMA((PIECES, turns, levels)),
            pltpu.SemaphoreType.DMA((PIECES, turns)),
            pltpu.SemaphoreType.DMA((levels,)),
            pltpu.SemaphoreType.DMA((levels,)),
            pltpu.SemaphoreType.DMA((GROUP, 2)),
            pltpu.SemaphoreType.DMA((GROUP, 2)),
            pltpu.SemaphoreType.DMA((n_head - 1, GROUP, share)),
            pltpu.SemaphoreType.DMA((n_head - 1, GROUP, share)),
            pltpu.SemaphoreType.DMA((GROUP, share)),
            pltpu.SemaphoreType.DMA((GROUP, share)),
        ],
        compiler_params=pltpu.CompilerParams(
            collective_id=0, has_side_effects=True, vmem_limit_bytes=56 * 1024 * 1024
        ),
    )(queries, keys, values, pool_weight, out_weight, pattern)


def solution(mesh):
    in_specs = (
        P("ctx", "head"),
        P("ctx", "head"),
        P("ctx", "head"),
        P("ctx", None),
        P("head", "ctx"),
        P(),
    )
    out_specs = P("ctx", "head")
    body = functools.partial(on_device, mesh.shape["ctx"], mesh.shape["head"])
    return jax.shard_map(
        body, mesh=mesh, in_specs=in_specs, out_specs=out_specs, check_vma=False
    )
```

```python
import functools

import jax
import jax.numpy as jnp
from jax import lax
from jax.experimental import pallas as pl
from jax.experimental.pallas import tpu as pltpu
from jax.sharding import PartitionSpec as P

HEAD_DIMENSION = 128
BLK = 128
NEAR_LEVELS = 1
MESH = pl.DeviceIdType.MESH
PIECES = 4
GROUP = 4


def flip_bit(index, step):
    return index + step - 2 * step * lax.rem(lax.div(index, step), 2)


def differing_bits(first, second, steps):
    total = 0
    for step in steps:
        a = lax.rem(lax.div(first, step), 2)
        b = lax.rem(lax.div(second, step), 2)
        total = total + step * (a + b - 2 * a * b)
    return total


def scores_of(queries, keys):
    return lax.dot_general(
        queries, keys, (((1,), (1,)), ((), ())), preferred_element_type=jnp.float32
    )


def layer_kernel(n_ctx, n_head, *refs):
    steps = [1 << bit for bit in range(n_ctx.bit_length() - 1)]
    levels = len(steps)
    q_ref, k_ref, v_ref, pool_ref, w_ref, pattern_ref, out_ref = refs[:7]
    refs = refs[7:]
    far_k, refs = refs[:levels], refs[levels:]
    far_v, refs = refs[:levels], refs[levels:]
    (w_buf, marks, acc, top, total, attended, partial, arrived, summed, shared) = refs[:10]
    (kv_send, kv_recv, w_send, w_recv, mark_send, mark_recv) = refs[10:16]
    (att_send, att_recv, head_send, head_recv, out_send, out_recv) = refs[16:]

    tok_rows, col_width = q_ref.shape
    heads = col_width // HEAD_DIMENSION
    blocks = tok_rows // BLK
    land = pool_ref.shape[0]
    depth, w_width = w_ref.shape
    piece_rows = depth // PIECES
    scale = HEAD_DIMENSION ** (-0.5)

    me = lax.axis_index("ctx")
    my_head = lax.axis_index("head")
    partner = {step: flip_bit(me, step) for step in steps}
    head_peer = [lax.rem(my_head + j, n_head) for j in range(n_head)]

    barrier = pltpu.get_barrier_semaphore()
    for step in steps:
        pl.semaphore_signal(barrier, inc=1, device_id={"ctx": partner[step]}, device_id_type=MESH)
    across = flip_bit(partner[1], 2)
    member = [me, partner[1], partner[2], across]
    pl.semaphore_signal(barrier, inc=1, device_id={"ctx": across}, device_id_type=MESH)
    for j in range(1, n_head):
        pl.semaphore_signal(barrier, inc=1, device_id={"head": head_peer[j]}, device_id_type=MESH)
    pl.semaphore_wait(barrier, levels + n_head)

    order = steps[2:][::-1]
    held = [[0]]
    for step in order:
        before = [r for stage in held for r in stage]
        held.append([r ^ step for r in before])
    open_sends = []

    def send_w(piece, r, stage):
        step = order[stage]
        rows = pl.ds(piece * piece_rows, piece_rows)
        source = w_ref.at[rows] if r == 0 else w_buf.at[r // GROUP, rows]
        copy = pltpu.make_async_remote_copy(
            src_ref=source,
            dst_ref=w_buf.at[(r ^ step) // GROUP, rows],
            send_sem=w_send.at[piece, r // GROUP, stage],
            recv_sem=w_recv.at[piece, (r ^ step) // GROUP],
            device_id={"ctx": partner[step]},
            device_id_type=MESH,
        )
        copy.start()
        open_sends.append(copy)

    def wait_w(piece, r):
        rows = pl.ds(piece * piece_rows, piece_rows)
        pltpu.make_async_remote_copy(
            src_ref=w_ref.at[rows],
            dst_ref=w_buf.at[r // GROUP, rows],
            send_sem=w_send.at[piece, 0, 0],
            recv_sem=w_recv.at[piece, r // GROUP],
            device_id={"ctx": partner[1]},
            device_id_type=MESH,
        ).wait_recv()

    def forward_w(stage):
        for r in held[stage + 1]:
            for piece in range(PIECES):
                wait_w(piece, r)
                for later in range(stage + 1, len(order)):
                    send_w(piece, r, later)

    kv_copies = {}

    def send_kv(level, which):
        source, target = ((k_ref, far_k[level]), (v_ref, far_v[level]))[which]
        copy = pltpu.make_async_remote_copy(
            src_ref=source,
            dst_ref=target,
            send_sem=kv_send.at[level, which],
            recv_sem=kv_recv.at[level, which],
            device_id={"ctx": partner[steps[level]]},
            device_id_type=MESH,
        )
        copy.start()
        kv_copies[level, which] = copy

    mark_copies = []

    def send_marks(stage):
        size = 1 << stage
        copy = pltpu.make_async_remote_copy(
            src_ref=marks.at[pl.ds(0, size)],
            dst_ref=marks.at[pl.ds(size, size)],
            send_sem=mark_send.at[stage],
            recv_sem=mark_recv.at[stage],
            device_id={"ctx": partner[steps[levels - 1 - stage]]},
            device_id_type=MESH,
        )
        copy.start()
        mark_copies.append(copy)

    def head_columns(head):
        return pl.ds(pl.multiple_of(head * HEAD_DIMENSION, HEAD_DIMENSION), HEAD_DIMENSION)

    def merge(entries):
        merged = []
        for head, rows, raw, value_set in entries:
            old_top = top[head, rows]
            new_top = jnp.maximum(old_top, jnp.max(raw, axis=-1, keepdims=True))
            weights = jnp.exp((raw - new_top) * scale)
            rescale = jnp.exp((old_top - new_top) * scale)
            new_total = total[head, rows] * rescale + jnp.sum(weights, axis=-1, keepdims=True)
            new_acc = acc[head, rows] * rescale + jnp.dot(
                weights.astype(jnp.bfloat16), value_set, preferred_element_type=jnp.float32
            )
            merged.append((new_top, new_total, new_acc))
        for (head, rows, _, _), (new_top, new_total, new_acc) in zip(entries, merged):
            top[head, rows] = new_top
            total[head, rows] = new_total
            acc[head, rows] = new_acc

    def near_attention():
        @pl.loop(0, heads // 2)
        def _(index):
            found = []
            for head in (index * 2, index * 2 + 1):
                columns = head_columns(head)
                raw = scores_of(q_ref[:, columns], k_ref[:, columns])
                row_top = jnp.max(raw, axis=-1, keepdims=True)
                weights = jnp.exp((raw - row_top) * scale)
                row_sum = jnp.sum(weights, axis=-1, keepdims=True)
                weighted = jnp.dot(
                    weights.astype(jnp.bfloat16),
                    v_ref[:, columns],
                    preferred_element_type=jnp.float32,
                )
                found.append((head, row_top, row_sum, weighted))
            for head, row_top, row_sum, weighted in found:
                top[head] = row_top
                total[head] = row_sum
                acc[head] = weighted

    def mark_attention():
        @pl.loop(0, heads // 2)
        def _(index):
            entries = []
            for head in (index * 2, index * 2 + 1):
                columns = head_columns(head)
                both = marks[:, :, columns].astype(jnp.float32)
                flat = (n_ctx * land, HEAD_DIMENSION)
                mark_keys = both[:, :land].reshape(flat).astype(jnp.bfloat16)
                mark_values = both[:, land:].reshape(flat).astype(jnp.bfloat16)
                raw = scores_of(q_ref[:, columns], mark_keys)
                entries.append((head, pl.ds(0, tok_rows), raw, mark_values))
            merge(entries)

    def chosen(ref, wanted, columns):
        picked = ref[pl.ds(0, BLK), columns]
        for block in range(1, blocks):
            other = ref[pl.ds(block * BLK, BLK), columns]
            picked = lax.select(wanted == block, other, picked)
        return picked

    def far_attention(level):
        first = partner[steps[level]] * blocks
        if level != levels - 1:
            for which in range(2):
                kv_copies[level, which].wait_recv()

        @pl.loop(0, heads // 4)
        def _(index):
            entries = []
            for extra in range(4):
                head = index * 4 + extra
                columns = head_columns(head)
                for block in range(blocks):
                    wanted = pattern_ref[me * blocks + block, NEAR_LEVELS + level] - first
                    rows = pl.ds(block * BLK, BLK)
                    far_keys = chosen(far_k[level], wanted, columns)
                    far_values = chosen(far_v[level], wanted, columns)
                    raw = scores_of(q_ref[rows, columns], far_keys)
                    entries.append((head, rows, raw, far_values))
            merge(entries)

    half = col_width // 2
    att_copies = {}

    def send_attended(source, piece, step):
        columns = pl.ds(piece * half, half)
        copy = pltpu.make_async_remote_copy(
            src_ref=attended.at[source, :, columns],
            dst_ref=attended.at[source ^ step, :, columns],
            send_sem=att_send.at[source ^ step, piece],
            recv_sem=att_recv.at[source ^ step, piece],
            device_id={"ctx": partner[step]},
            device_id_type=MESH,
        )
        copy.start()
        att_copies[source ^ step, piece] = copy

    pooled = [
        jnp.dot(pool_ref[...], ref[...], preferred_element_type=jnp.float32) for ref in (k_ref, v_ref)
    ]
    marks[0] = jnp.concatenate(pooled, axis=0).astype(jnp.bfloat16)
    send_marks(0)
    for which in range(2):
        for level in range(levels)[::-1]:
            send_kv(level, which)

    near_attention()
    mark_copies[0].wait_recv()
    send_marks(1)
    far_attention(0)
    far_attention(1)
    for which in range(2):
        kv_copies[levels - 1, which].wait_recv()
    for stage in range(len(order)):
        for piece in range(PIECES):
            send_w(piece, 0, stage)
    for stage in range(2, levels):
        mark_copies[stage - 1].wait_recv()
        send_marks(stage)
        far_attention(levels + 1 - stage)
    mark_copies[levels - 1].wait_recv()
    mark_attention()

    @pl.loop(0, heads)
    def _(head):
        attended[0, :, head_columns(head)] = (acc[head] / total[head]).astype(jnp.bfloat16)

    for piece in range(2):
        for step in (1 << piece, 2 >> piece):
            send_attended(0, piece, step)
    for piece in range(2):
        att_copies[1 << piece, piece].wait_recv()
        send_attended(1 << piece, piece, 2 >> piece)
    for stage in range(len(order) - 1):
        forward_w(stage)
    for piece in range(2):
        att_copies[2 >> piece, piece].wait_recv()
        att_copies[3, piece].wait_recv()

    turns = n_ctx // GROUP
    share = turns // n_head

    def project(r):
        turn = lax.div(differing_bits(me, r, steps), GROUP)

        @pl.loop(0, GROUP)
        def _(index):
            columns = w_ref[...] if r == 0 else w_buf[r // GROUP]
            rows = jnp.dot(attended[index], columns, preferred_element_type=jnp.float32)
            partial[index, turn] = rows.astype(jnp.bfloat16)

    my_turn = lax.div(me, GROUP)
    bits = [1 << bit for bit in range(turns.bit_length() - 1)]
    low_bits = [bit for bit in bits if bit < share]
    head_copies = {}
    out_copies = []

    def send_partials(low, turn):
        for index in range(GROUP)[::-1]:
            for j in range(1, n_head):
                copy = pltpu.make_async_remote_copy(
                    src_ref=partial.at[index, head_peer[j] * share + turn],
                    dst_ref=arrived.at[j - 1, index, turn],
                    send_sem=head_send.at[j - 1, index, low],
                    recv_sem=head_recv.at[j - 1, index, low],
                    device_id={"head": head_peer[j]},
                    device_id_type=MESH,
                )
                copy.start()
                head_copies[index, j, low] = copy

    def send_sums(low, turn):
        for index in range(GROUP)[::-1]:
            mixed = partial[index, my_head * share + turn].astype(jnp.float32)
            for j in range(1, n_head):
                head_copies[index, j, low].wait_recv()
                mixed += arrived[j - 1, index, turn].astype(jnp.float32)
            target = summed if index else shared
            target[index, turn] = mixed.astype(jnp.bfloat16)
            if index:
                copy = pltpu.make_async_remote_copy(
                    src_ref=summed.at[index, turn],
                    dst_ref=shared.at[index, turn],
                    send_sem=out_send.at[index, low],
                    recv_sem=out_recv.at[index, low],
                    device_id={"ctx": member[index]},
                    device_id_type=MESH,
                )
                copy.start()
                out_copies.append(copy)

    late = set(held[len(order)])
    everything = [r for stage in held for r in stage]
    for low in range(share):
        turn = differing_bits(lax.rem(my_turn, share), low, low_bits)
        for r in everything:
            if (r // GROUP) % share == low:
                if r in late:
                    for piece in range(PIECES):
                        wait_w(piece, r)
                project(r)
        send_partials(low, turn)
        send_sums(low, turn)
    for copy in out_copies:
        copy.wait_recv()

    pair = max(1, 128 // w_width)
    for first in range(0, share * GROUP, pair):
        parts = []
        for slot in range(first, first + pair):
            index = differing_bits(lax.rem(me, GROUP), slot % GROUP, (1, 2))
            parts.append(shared[index, slot // GROUP])
        whole = parts[0] if pair == 1 else jnp.concatenate(parts, axis=1)
        out_ref[:, pl.ds(first * w_width, pair * w_width)] = whole

    sent = open_sends + mark_copies + out_copies
    for copies in (kv_copies, att_copies, head_copies):
        sent.extend(copies.values())
    for copy in sent:
        copy.wait_send()


def on_device(n_ctx, n_head, queries, keys, values, pool_weight, out_weight, pattern):
    tok_rows, col_width = queries.shape
    heads = col_width // HEAD_DIMENSION
    depth, w_width = out_weight.shape
    land = pool_weight.shape[0]
    levels = n_ctx.bit_length() - 1
    turns = n_ctx // GROUP
    share = turns // n_head
    bf16 = jnp.bfloat16
    in_vmem = pl.BlockSpec(memory_space=pltpu.VMEM)
    return pl.pallas_call(
        functools.partial(layer_kernel, n_ctx, n_head),
        out_shape=jax.ShapeDtypeStruct((tok_rows, share * GROUP * w_width), bf16),
        in_specs=[in_vmem] * 5 + [pl.BlockSpec(memory_space=pltpu.SMEM)],
        out_specs=in_vmem,
        scratch_shapes=[pltpu.VMEM((tok_rows, col_width), bf16)] * (2 * levels)
        + [
            pltpu.VMEM((turns, depth, w_width), bf16),
            pltpu.VMEM((n_ctx, 2 * land, col_width), bf16),
            pltpu.VMEM((heads, tok_rows, HEAD_DIMENSION), jnp.float32),
            pltpu.VMEM((heads, tok_rows, 1), jnp.float32),
            pltpu.VMEM((heads, tok_rows, 1), jnp.float32),
            pltpu.VMEM((GROUP, tok_rows, col_width), bf16),
            pltpu.VMEM((GROUP, turns, tok_rows, w_width), bf16),
            pltpu.VMEM((n_head - 1, GROUP, share, tok_rows, w_width), bf16),
            pltpu.VMEM((GROUP, share, tok_rows, w_width), bf16),
            pltpu.VMEM((GROUP, share, tok_rows, w_width), bf16),
            pltpu.SemaphoreType.DMA((levels, 2)),
            pltpu.SemaphoreType.DMA((levels, 2)),
            pltpu.SemaphoreType.DMA((PIECES, turns, levels)),
            pltpu.SemaphoreType.DMA((PIECES, turns)),
            pltpu.SemaphoreType.DMA((levels,)),
            pltpu.SemaphoreType.DMA((levels,)),
            pltpu.SemaphoreType.DMA((GROUP, 2)),
            pltpu.SemaphoreType.DMA((GROUP, 2)),
            pltpu.SemaphoreType.DMA((n_head - 1, GROUP, share)),
            pltpu.SemaphoreType.DMA((n_head - 1, GROUP, share)),
            pltpu.SemaphoreType.DMA((GROUP, share)),
            pltpu.SemaphoreType.DMA((GROUP, share)),
        ],
        compiler_params=pltpu.CompilerParams(
            collective_id=0, has_side_effects=True, vmem_limit_bytes=56 * 1024 * 1024
        ),
    )(queries, keys, values, pool_weight, out_weight, pattern)


def solution(mesh):
    in_specs = (
        P("ctx", "head"),
        P("ctx", "head"),
        P("ctx", "head"),
        P("ctx", None),
        P("head", "ctx"),
        P(),
    )
    out_specs = P("ctx", "head")
    body = functools.partial(on_device, mesh.shape["ctx"], mesh.shape["head"])
    return jax.shard_map(
        body, mesh=mesh, in_specs=in_specs, out_specs=out_specs, check_vma=False
    )
```

```python
import functools

import jax
import jax.numpy as jnp
from jax import lax
from jax.experimental import pallas as pl
from jax.experimental.pallas import tpu as pltpu
from jax.sharding import PartitionSpec as P

HEAD_DIMENSION = 128
BLK = 128
NEAR_LEVELS = 1
MESH = pl.DeviceIdType.MESH
PIECES = 4
GROUP = 4


def flip_bit(index, step):
    return index + step - 2 * step * lax.rem(lax.div(index, step), 2)


def differing_bits(first, second, steps):
    total = 0
    for step in steps:
        a = lax.rem(lax.div(first, step), 2)
        b = lax.rem(lax.div(second, step), 2)
        total = total + step * (a + b - 2 * a * b)
    return total


def scores_of(queries, keys):
    return lax.dot_general(
        queries, keys, (((1,), (1,)), ((), ())), preferred_element_type=jnp.float32
    )


def layer_kernel(n_ctx, n_head, *refs):
    steps = [1 << bit for bit in range(n_ctx.bit_length() - 1)]
    levels = len(steps)
    q_ref, k_hbm, v_hbm, pool_ref, w_ref, pattern_ref, out_ref, k_ref, v_ref = refs[:9]
    refs = refs[9:]
    far_k, refs = refs[:levels], refs[levels:]
    far_v, refs = refs[:levels], refs[levels:]
    (w_buf, marks, acc, top, total, attended, partial, arrived, summed, shared) = refs[:10]
    (kv_send, kv_recv, w_send, w_recv, mark_send, mark_recv) = refs[10:16]
    (att_send, att_recv, head_send, head_recv, out_send, out_recv, near_sem) = refs[16:]

    tok_rows, col_width = q_ref.shape
    heads = col_width // HEAD_DIMENSION
    blocks = tok_rows // BLK
    land = pool_ref.shape[0]
    depth, w_width = w_ref.shape
    piece_rows = depth // PIECES
    scale = HEAD_DIMENSION ** (-0.5)

    me = lax.axis_index("ctx")
    my_head = lax.axis_index("head")
    partner = {step: flip_bit(me, step) for step in steps}
    head_peer = [lax.rem(my_head + j, n_head) for j in range(n_head)]

    barrier = pltpu.get_barrier_semaphore()
    for step in steps:
        pl.semaphore_signal(barrier, inc=1, device_id={"ctx": partner[step]}, device_id_type=MESH)
    across = flip_bit(partner[1], 2)
    member = [me, partner[1], partner[2], across]
    pl.semaphore_signal(barrier, inc=1, device_id={"ctx": across}, device_id_type=MESH)
    for j in range(1, n_head):
        pl.semaphore_signal(barrier, inc=1, device_id={"head": head_peer[j]}, device_id_type=MESH)
    pl.semaphore_wait(barrier, levels + n_head)

    order = steps[2:][::-1]
    held = [[0]]
    for step in order:
        before = [r for stage in held for r in stage]
        held.append([r ^ step for r in before])
    open_sends = []

    def send_w(piece, r, stage):
        step = order[stage]
        rows = pl.ds(piece * piece_rows, piece_rows)
        source = w_ref.at[rows] if r == 0 else w_buf.at[r // GROUP, rows]
        copy = pltpu.make_async_remote_copy(
            src_ref=source,
            dst_ref=w_buf.at[(r ^ step) // GROUP, rows],
            send_sem=w_send.at[piece, r // GROUP, stage],
            recv_sem=w_recv.at[piece, (r ^ step) // GROUP],
            device_id={"ctx": partner[step]},
            device_id_type=MESH,
        )
        copy.start()
        open_sends.append(copy)

    def wait_w(piece, r):
        rows = pl.ds(piece * piece_rows, piece_rows)
        pltpu.make_async_remote_copy(
            src_ref=w_ref.at[rows],
            dst_ref=w_buf.at[r // GROUP, rows],
            send_sem=w_send.at[piece, 0, 0],
            recv_sem=w_recv.at[piece, r // GROUP],
            device_id={"ctx": partner[1]},
            device_id_type=MESH,
        ).wait_recv()

    def forward_w(stage):
        for r in held[stage + 1]:
            for piece in range(PIECES):
                wait_w(piece, r)
                for later in range(stage + 1, len(order)):
                    send_w(piece, r, later)

    kv_copies = {}

    def send_kv(level, which):
        source, target = ((k_hbm, far_k[level]), (v_hbm, far_v[level]))[which]
        copy = pltpu.make_async_remote_copy(
            src_ref=source,
            dst_ref=target,
            send_sem=kv_send.at[level, which],
            recv_sem=kv_recv.at[level, which],
            device_id={"ctx": partner[steps[level]]},
            device_id_type=MESH,
        )
        copy.start()
        kv_copies[level, which] = copy

    mark_copies = []

    def send_marks(stage):
        size = 1 << stage
        copy = pltpu.make_async_remote_copy(
            src_ref=marks.at[pl.ds(0, size)],
            dst_ref=marks.at[pl.ds(size, size)],
            send_sem=mark_send.at[stage],
            recv_sem=mark_recv.at[stage],
            device_id={"ctx": partner[steps[levels - 1 - stage]]},
            device_id_type=MESH,
        )
        copy.start()
        mark_copies.append(copy)

    def head_columns(head):
        return pl.ds(pl.multiple_of(head * HEAD_DIMENSION, HEAD_DIMENSION), HEAD_DIMENSION)

    def merge(entries):
        merged = []
        for head, rows, raw, value_set in entries:
            old_top = top[head, rows]
            new_top = jnp.maximum(old_top, jnp.max(raw, axis=-1, keepdims=True))
            weights = jnp.exp((raw - new_top) * scale)
            rescale = jnp.exp((old_top - new_top) * scale)
            new_total = total[head, rows] * rescale + jnp.sum(weights, axis=-1, keepdims=True)
            new_acc = acc[head, rows] * rescale + jnp.dot(
                weights.astype(jnp.bfloat16), value_set, preferred_element_type=jnp.float32
            )
            merged.append((new_top, new_total, new_acc))
        for (head, rows, _, _), (new_top, new_total, new_acc) in zip(entries, merged):
            top[head, rows] = new_top
            total[head, rows] = new_total
            acc[head, rows] = new_acc

    def near_attention():
        @pl.loop(0, heads // 2)
        def _(index):
            found = []
            for head in (index * 2, index * 2 + 1):
                columns = head_columns(head)
                raw = scores_of(q_ref[:, columns], k_ref[:, columns])
                row_top = jnp.max(raw, axis=-1, keepdims=True)
                weights = jnp.exp((raw - row_top) * scale)
                row_sum = jnp.sum(weights, axis=-1, keepdims=True)
                weighted = jnp.dot(
                    weights.astype(jnp.bfloat16),
                    v_ref[:, columns],
                    preferred_element_type=jnp.float32,
                )
                found.append((head, row_top, row_sum, weighted))
            for head, row_top, row_sum, weighted in found:
                top[head] = row_top
                total[head] = row_sum
                acc[head] = weighted

    def mark_attention():
        @pl.loop(0, heads // 2)
        def _(index):
            entries = []
            for head in (index * 2, index * 2 + 1):
                columns = head_columns(head)
                both = marks[:, :, columns].astype(jnp.float32)
                flat = (n_ctx * land, HEAD_DIMENSION)
                mark_keys = both[:, :land].reshape(flat).astype(jnp.bfloat16)
                mark_values = both[:, land:].reshape(flat).astype(jnp.bfloat16)
                raw = scores_of(q_ref[:, columns], mark_keys)
                entries.append((head, pl.ds(0, tok_rows), raw, mark_values))
            merge(entries)

    def chosen(ref, wanted, columns):
        picked = ref[pl.ds(0, BLK), columns]
        for block in range(1, blocks):
            other = ref[pl.ds(block * BLK, BLK), columns]
            picked = lax.select(wanted == block, other, picked)
        return picked

    def far_attention(level):
        first = partner[steps[level]] * blocks
        for which in range(2):
            if (level, which) != (levels - 1, 0):
                kv_copies[level, which].wait_recv()

        @pl.loop(0, heads // 4)
        def _(index):
            entries = []
            for extra in range(4):
                head = index * 4 + extra
                columns = head_columns(head)
                for block in range(blocks):
                    wanted = pattern_ref[me * blocks + block, NEAR_LEVELS + level] - first
                    rows = pl.ds(block * BLK, BLK)
                    far_keys = chosen(far_k[level], wanted, columns)
                    far_values = chosen(far_v[level], wanted, columns)
                    raw = scores_of(q_ref[rows, columns], far_keys)
                    entries.append((head, rows, raw, far_values))
            merge(entries)

    half = col_width // 2
    att_copies = {}

    def send_attended(source, piece, step):
        columns = pl.ds(piece * half, half)
        copy = pltpu.make_async_remote_copy(
            src_ref=attended.at[source, :, columns],
            dst_ref=attended.at[source ^ step, :, columns],
            send_sem=att_send.at[source ^ step, piece],
            recv_sem=att_recv.at[source ^ step, piece],
            device_id={"ctx": partner[step]},
            device_id_type=MESH,
        )
        copy.start()
        att_copies[source ^ step, piece] = copy

    for level in range(2, levels)[::-1]:
        send_kv(level, 0)
    near_copies = [
        pltpu.make_async_copy(source, target, near_sem.at[which])
        for which, (source, target) in enumerate(((k_hbm, k_ref), (v_hbm, v_ref)))
    ]
    for copy in near_copies:
        copy.start()
    for level in range(2):
        send_kv(level, 0)
    for copy in near_copies:
        copy.wait()
    pooled = [
        jnp.dot(pool_ref[...], ref[...], preferred_element_type=jnp.float32) for ref in (k_ref, v_ref)
    ]
    marks[0] = jnp.concatenate(pooled, axis=0).astype(jnp.bfloat16)
    send_marks(0)
    for level in range(levels)[::-1]:
        send_kv(level, 1)

    own_copy = pltpu.make_async_copy(w_ref, w_buf.at[0], near_sem.at[2])
    own_copy.start()
    near_attention()
    own_copy.wait()
    mark_copies[0].wait_recv()
    send_marks(1)
    far_attention(0)
    far_attention(1)
    kv_copies[levels - 1, 0].wait_recv()
    for stage in range(len(order)):
        for piece in range(PIECES):
            send_w(piece, 0, stage)
    for stage in range(2, levels):
        mark_copies[stage - 1].wait_recv()
        send_marks(stage)
        far_attention(levels + 1 - stage)
    mark_copies[levels - 1].wait_recv()
    mark_attention()

    @pl.loop(0, heads)
    def _(head):
        attended[0, :, head_columns(head)] = (acc[head] / total[head]).astype(jnp.bfloat16)

    for piece in range(2):
        for step in (1 << piece, 2 >> piece):
            send_attended(0, piece, step)
    for piece in range(2):
        att_copies[1 << piece, piece].wait_recv()
        send_attended(1 << piece, piece, 2 >> piece)
    for stage in range(len(order) - 1):
        forward_w(stage)
    for piece in range(2):
        att_copies[2 >> piece, piece].wait_recv()
        att_copies[3, piece].wait_recv()

    turns = n_ctx // GROUP
    share = turns // n_head

    def project(r):
        turn = lax.div(differing_bits(me, r, steps), GROUP)

        @pl.loop(0, GROUP)
        def _(index):
            rows = jnp.dot(
                attended[index], w_buf[r // GROUP], preferred_element_type=jnp.float32
            )
            partial[index, turn] = rows.astype(jnp.bfloat16)

    my_turn = lax.div(me, GROUP)
    bits = [1 << bit for bit in range(turns.bit_length() - 1)]
    low_bits = [bit for bit in bits if bit < share]
    head_copies = {}
    out_copies = []

    def send_partials(low, turn):
        for index in range(GROUP)[::-1]:
            for j in range(1, n_head):
                copy = pltpu.make_async_remote_copy(
                    src_ref=partial.at[index, head_peer[j] * share + turn],
                    dst_ref=arrived.at[j - 1, index, turn],
                    send_sem=head_send.at[j - 1, index, low],
                    recv_sem=head_recv.at[j - 1, index, low],
                    device_id={"head": head_peer[j]},
                    device_id_type=MESH,
                )
                copy.start()
                head_copies[index, j, low] = copy

    def send_sums(low, turn):
        for index in range(GROUP)[::-1]:
            mixed = partial[index, my_head * share + turn].astype(jnp.float32)
            for j in range(1, n_head):
                head_copies[index, j, low].wait_recv()
                mixed += arrived[j - 1, index, turn].astype(jnp.float32)
            target = summed if index else shared
            target[index, turn] = mixed.astype(jnp.bfloat16)
            if index:
                copy = pltpu.make_async_remote_copy(
                    src_ref=summed.at[index, turn],
                    dst_ref=shared.at[index, turn],
                    send_sem=out_send.at[index, low],
                    recv_sem=out_recv.at[index, low],
                    device_id={"ctx": member[index]},
                    device_id_type=MESH,
                )
                copy.start()
                out_copies.append(copy)

    late = set(held[len(order)])
    everything = [r for stage in held for r in stage]
    for low in range(share):
        turn = differing_bits(lax.rem(my_turn, share), low, low_bits)
        for r in everything:
            if (r // GROUP) % share == low:
                if r in late:
                    for piece in range(PIECES):
                        wait_w(piece, r)
                project(r)
        send_partials(low, turn)
        send_sums(low, turn)
    for copy in out_copies:
        copy.wait_recv()

    pair = max(1, 128 // w_width)
    for first in range(0, share * GROUP, pair):
        parts = []
        for slot in range(first, first + pair):
            index = differing_bits(lax.rem(me, GROUP), slot % GROUP, (1, 2))
            parts.append(shared[index, slot // GROUP])
        whole = parts[0] if pair == 1 else jnp.concatenate(parts, axis=1)
        out_ref[:, pl.ds(first * w_width, pair * w_width)] = whole

    sent = open_sends + mark_copies + out_copies
    for copies in (kv_copies, att_copies, head_copies):
        sent.extend(copies.values())
    for copy in sent:
        copy.wait_send()


def on_device(n_ctx, n_head, queries, keys, values, pool_weight, out_weight, pattern):
    tok_rows, col_width = queries.shape
    heads = col_width // HEAD_DIMENSION
    depth, w_width = out_weight.shape
    land = pool_weight.shape[0]
    levels = n_ctx.bit_length() - 1
    turns = n_ctx // GROUP
    share = turns // n_head
    bf16 = jnp.bfloat16
    in_vmem = pl.BlockSpec(memory_space=pltpu.VMEM)
    in_place = pl.BlockSpec(memory_space=pl.ANY)
    return pl.pallas_call(
        functools.partial(layer_kernel, n_ctx, n_head),
        out_shape=jax.ShapeDtypeStruct((tok_rows, share * GROUP * w_width), bf16),
        in_specs=[in_vmem, in_place, in_place, in_vmem, in_place]
        + [pl.BlockSpec(memory_space=pltpu.SMEM)],
        out_specs=in_vmem,
        scratch_shapes=[pltpu.VMEM((tok_rows, col_width), bf16)] * (2 * levels + 2)
        + [
            pltpu.VMEM((turns, depth, w_width), bf16),
            pltpu.VMEM((n_ctx, 2 * land, col_width), bf16),
            pltpu.VMEM((heads, tok_rows, HEAD_DIMENSION), jnp.float32),
            pltpu.VMEM((heads, tok_rows, 1), jnp.float32),
            pltpu.VMEM((heads, tok_rows, 1), jnp.float32),
            pltpu.VMEM((GROUP, tok_rows, col_width), bf16),
            pltpu.VMEM((GROUP, turns, tok_rows, w_width), bf16),
            pltpu.VMEM((n_head - 1, GROUP, share, tok_rows, w_width), bf16),
            pltpu.VMEM((GROUP, share, tok_rows, w_width), bf16),
            pltpu.VMEM((GROUP, share, tok_rows, w_width), bf16),
            pltpu.SemaphoreType.DMA((levels, 2)),
            pltpu.SemaphoreType.DMA((levels, 2)),
            pltpu.SemaphoreType.DMA((PIECES, turns, levels)),
            pltpu.SemaphoreType.DMA((PIECES, turns)),
            pltpu.SemaphoreType.DMA((levels,)),
            pltpu.SemaphoreType.DMA((levels,)),
            pltpu.SemaphoreType.DMA((GROUP, 2)),
            pltpu.SemaphoreType.DMA((GROUP, 2)),
            pltpu.SemaphoreType.DMA((n_head - 1, GROUP, share)),
            pltpu.SemaphoreType.DMA((n_head - 1, GROUP, share)),
            pltpu.SemaphoreType.DMA((GROUP, share)),
            pltpu.SemaphoreType.DMA((GROUP, share)),
            pltpu.SemaphoreType.DMA((3,)),
        ],
        compiler_params=pltpu.CompilerParams(
            collective_id=0, has_side_effects=True, vmem_limit_bytes=56 * 1024 * 1024
        ),
    )(queries, keys, values, pool_weight, out_weight, pattern)


def solution(mesh):
    in_specs = (
        P("ctx", "head"),
        P("ctx", "head"),
        P("ctx", "head"),
        P("ctx", None),
        P("head", "ctx"),
        P(),
    )
    out_specs = P("ctx", "head")
    body = functools.partial(on_device, mesh.shape["ctx"], mesh.shape["head"])
    return jax.shard_map(
        body, mesh=mesh, in_specs=in_specs, out_specs=out_specs, check_vma=False
    )
```

```python
import functools

import jax
import jax.numpy as jnp
from jax import lax
from jax.experimental import pallas as pl
from jax.experimental.pallas import tpu as pltpu
from jax.sharding import PartitionSpec as P

HEAD_DIMENSION = 128
BLK = 128
NEAR_LEVELS = 1
MESH = pl.DeviceIdType.MESH
PIECES = 4
GROUP = 4


def flip_bit(index, step):
    return index + step - 2 * step * lax.rem(lax.div(index, step), 2)


def differing_bits(first, second, steps):
    total = 0
    for step in steps:
        a = lax.rem(lax.div(first, step), 2)
        b = lax.rem(lax.div(second, step), 2)
        total = total + step * (a + b - 2 * a * b)
    return total


def scores_of(queries, keys):
    return lax.dot_general(
        queries, keys, (((1,), (1,)), ((), ())), preferred_element_type=jnp.float32
    )


def layer_kernel(n_ctx, n_head, *refs):
    steps = [1 << bit for bit in range(n_ctx.bit_length() - 1)]
    levels = len(steps)
    q_ref, k_hbm, v_hbm, pool_ref, w_ref, pattern_ref, out_ref, k_ref, v_ref = refs[:9]
    refs = refs[9:]
    far_k, refs = refs[:levels], refs[levels:]
    far_v, refs = refs[:levels], refs[levels:]
    (w_buf, marks, acc, top, total, attended, partial, arrived, summed, shared) = refs[:10]
    (kv_send, kv_recv, w_send, w_recv, mark_send, mark_recv) = refs[10:16]
    (att_send, att_recv, head_send, head_recv, out_send, out_recv, near_sem) = refs[16:]

    tok_rows, col_width = q_ref.shape
    heads = col_width // HEAD_DIMENSION
    blocks = tok_rows // BLK
    land = pool_ref.shape[0]
    depth, w_width = w_ref.shape
    piece_rows = depth // PIECES
    scale = HEAD_DIMENSION ** (-0.5)

    me = lax.axis_index("ctx")
    my_head = lax.axis_index("head")
    partner = {step: flip_bit(me, step) for step in steps}
    head_peer = [lax.rem(my_head + j, n_head) for j in range(n_head)]

    barrier = pltpu.get_barrier_semaphore()
    for step in steps:
        pl.semaphore_signal(barrier, inc=1, device_id={"ctx": partner[step]}, device_id_type=MESH)
    across = flip_bit(partner[1], 2)
    member = [me, partner[1], partner[2], across]
    pl.semaphore_signal(barrier, inc=1, device_id={"ctx": across}, device_id_type=MESH)
    for j in range(1, n_head):
        pl.semaphore_signal(barrier, inc=1, device_id={"head": head_peer[j]}, device_id_type=MESH)
    pl.semaphore_wait(barrier, levels + n_head)

    order = steps[2:][::-1]
    held = [[0]]
    for step in order:
        before = [r for stage in held for r in stage]
        held.append([r ^ step for r in before])
    open_sends = []

    def send_w(piece, r, stage):
        step = order[stage]
        rows = pl.ds(piece * piece_rows, piece_rows)
        source = w_ref.at[rows] if r == 0 else w_buf.at[r // GROUP, rows]
        copy = pltpu.make_async_remote_copy(
            src_ref=source,
            dst_ref=w_buf.at[(r ^ step) // GROUP, rows],
            send_sem=w_send.at[piece, r // GROUP, stage],
            recv_sem=w_recv.at[piece, (r ^ step) // GROUP],
            device_id={"ctx": partner[step]},
            device_id_type=MESH,
        )
        copy.start()
        open_sends.append(copy)

    def wait_w(piece, r):
        rows = pl.ds(piece * piece_rows, piece_rows)
        pltpu.make_async_remote_copy(
            src_ref=w_ref.at[rows],
            dst_ref=w_buf.at[r // GROUP, rows],
            send_sem=w_send.at[piece, 0, 0],
            recv_sem=w_recv.at[piece, r // GROUP],
            device_id={"ctx": partner[1]},
            device_id_type=MESH,
        ).wait_recv()

    def forward_w(stage):
        for r in held[stage + 1]:
            for piece in range(PIECES):
                wait_w(piece, r)
                for later in range(stage + 1, len(order)):
                    send_w(piece, r, later)

    kv_copies = {}

    def send_kv(level, which):
        source, target = ((k_hbm, far_k[level]), (v_hbm, far_v[level]))[which]
        copy = pltpu.make_async_remote_copy(
            src_ref=source,
            dst_ref=target,
            send_sem=kv_send.at[level, which],
            recv_sem=kv_recv.at[level, which],
            device_id={"ctx": partner[steps[level]]},
            device_id_type=MESH,
        )
        copy.start()
        kv_copies[level, which] = copy

    mark_copies = []

    def send_marks(stage):
        size = 1 << stage
        copy = pltpu.make_async_remote_copy(
            src_ref=marks.at[pl.ds(0, size)],
            dst_ref=marks.at[pl.ds(size, size)],
            send_sem=mark_send.at[stage],
            recv_sem=mark_recv.at[stage],
            device_id={"ctx": partner[steps[levels - 1 - stage]]},
            device_id_type=MESH,
        )
        copy.start()
        mark_copies.append(copy)

    def head_columns(head):
        return pl.ds(pl.multiple_of(head * HEAD_DIMENSION, HEAD_DIMENSION), HEAD_DIMENSION)

    def merge(entries):
        merged = []
        for head, rows, raw, value_set in entries:
            old_top = top[head, rows]
            new_top = jnp.maximum(old_top, jnp.max(raw, axis=-1, keepdims=True))
            weights = jnp.exp((raw - new_top) * scale)
            rescale = jnp.exp((old_top - new_top) * scale)
            new_total = total[head, rows] * rescale + jnp.sum(weights, axis=-1, keepdims=True)
            new_acc = acc[head, rows] * rescale + jnp.dot(
                weights.astype(jnp.bfloat16), value_set, preferred_element_type=jnp.float32
            )
            merged.append((new_top, new_total, new_acc))
        for (head, rows, _, _), (new_top, new_total, new_acc) in zip(entries, merged):
            top[head, rows] = new_top
            total[head, rows] = new_total
            acc[head, rows] = new_acc

    def near_attention():
        @pl.loop(0, heads // 2)
        def _(index):
            found = []
            for head in (index * 2, index * 2 + 1):
                columns = head_columns(head)
                raw = scores_of(q_ref[:, columns], k_ref[:, columns])
                row_top = jnp.max(raw, axis=-1, keepdims=True)
                weights = jnp.exp((raw - row_top) * scale)
                row_sum = jnp.sum(weights, axis=-1, keepdims=True)
                weighted = jnp.dot(
                    weights.astype(jnp.bfloat16),
                    v_ref[:, columns],
                    preferred_element_type=jnp.float32,
                )
                found.append((head, row_top, row_sum, weighted))
            for head, row_top, row_sum, weighted in found:
                top[head] = row_top
                total[head] = row_sum
                acc[head] = weighted

    def mark_attention():
        @pl.loop(0, heads // 2)
        def _(index):
            entries = []
            for head in (index * 2, index * 2 + 1):
                columns = head_columns(head)
                both = marks[:, :, columns].astype(jnp.float32)
                flat = (n_ctx * land, HEAD_DIMENSION)
                mark_keys = both[:, :land].reshape(flat).astype(jnp.bfloat16)
                mark_values = both[:, land:].reshape(flat).astype(jnp.bfloat16)
                raw = scores_of(q_ref[:, columns], mark_keys)
                entries.append((head, pl.ds(0, tok_rows), raw, mark_values))
            merge(entries)

    def chosen(ref, wanted, columns):
        picked = ref[pl.ds(0, BLK), columns]
        for block in range(1, blocks):
            other = ref[pl.ds(block * BLK, BLK), columns]
            picked = lax.select(wanted == block, other, picked)
        return picked

    def far_attention(level):
        first = partner[steps[level]] * blocks
        for which in range(2):
            if (level, which) != (levels - 1, 0):
                kv_copies[level, which].wait_recv()

        @pl.loop(0, heads // 4)
        def _(index):
            entries = []
            for extra in range(4):
                head = index * 4 + extra
                columns = head_columns(head)
                for block in range(blocks):
                    wanted = pattern_ref[me * blocks + block, NEAR_LEVELS + level] - first
                    rows = pl.ds(block * BLK, BLK)
                    far_keys = chosen(far_k[level], wanted, columns)
                    far_values = chosen(far_v[level], wanted, columns)
                    raw = scores_of(q_ref[rows, columns], far_keys)
                    entries.append((head, rows, raw, far_values))
            merge(entries)

    half = col_width // 2
    att_copies = {}

    def send_attended(source, piece, step):
        columns = pl.ds(piece * half, half)
        copy = pltpu.make_async_remote_copy(
            src_ref=attended.at[source, :, columns],
            dst_ref=attended.at[source ^ step, :, columns],
            send_sem=att_send.at[source ^ step, piece],
            recv_sem=att_recv.at[source ^ step, piece],
            device_id={"ctx": partner[step]},
            device_id_type=MESH,
        )
        copy.start()
        att_copies[source ^ step, piece] = copy

    for level in range(2, levels)[::-1]:
        send_kv(level, 0)
    near_copies = [
        pltpu.make_async_copy(source, target, near_sem.at[which])
        for which, (source, target) in enumerate(((k_hbm, k_ref), (v_hbm, v_ref)))
    ]
    for copy in near_copies:
        copy.start()
    for level in range(2):
        send_kv(level, 0)
    for copy in near_copies:
        copy.wait()
    pooled = [
        jnp.dot(pool_ref[...], ref[...], preferred_element_type=jnp.float32) for ref in (k_ref, v_ref)
    ]
    marks[0] = jnp.concatenate(pooled, axis=0).astype(jnp.bfloat16)
    send_marks(0)
    for level in range(levels)[::-1]:
        send_kv(level, 1)

    own_copy = pltpu.make_async_copy(w_ref, w_buf.at[0], near_sem.at[2])
    own_copy.start()
    near_attention()
    own_copy.wait()
    mark_copies[0].wait_recv()
    send_marks(1)
    far_attention(0)
    far_attention(1)
    kv_copies[levels - 1, 0].wait_recv()
    for stage in range(len(order)):
        for piece in range(PIECES):
            send_w(piece, 0, stage)
    for stage in range(2, levels):
        mark_copies[stage - 1].wait_recv()
        send_marks(stage)
        far_attention(levels + 1 - stage)
    mark_copies[levels - 1].wait_recv()
    mark_attention()

    @pl.loop(0, heads)
    def _(head):
        attended[0, :, head_columns(head)] = (acc[head] / total[head]).astype(jnp.bfloat16)

    for piece in range(2):
        for step in (1 << piece, 2 >> piece):
            send_attended(0, piece, step)
    for piece in range(2):
        att_copies[1 << piece, piece].wait_recv()
        send_attended(1 << piece, piece, 2 >> piece)
    for stage in range(len(order) - 1):
        forward_w(stage)
    for piece in range(2):
        att_copies[2 >> piece, piece].wait_recv()
        att_copies[3, piece].wait_recv()

    turns = n_ctx // GROUP
    share = turns // n_head

    def project_rows(r, index):
        turn = lax.div(differing_bits(me, r, steps), GROUP)
        rows = jnp.dot(attended[index], w_buf[r // GROUP], preferred_element_type=jnp.float32)
        partial[index, turn] = rows.astype(jnp.bfloat16)

    def project(r):
        @pl.loop(0, GROUP)
        def _(index):
            project_rows(r, index)

    my_turn = lax.div(me, GROUP)
    bits = [1 << bit for bit in range(turns.bit_length() - 1)]
    low_bits = [bit for bit in bits if bit < share]
    head_copies = {}
    out_copies = []

    def send_partials(low, turn, last):
        for index in range(GROUP)[::-1]:
            project_rows(last, index)
            for j in range(1, n_head):
                copy = pltpu.make_async_remote_copy(
                    src_ref=partial.at[index, head_peer[j] * share + turn],
                    dst_ref=arrived.at[j - 1, index, turn],
                    send_sem=head_send.at[j - 1, index, low],
                    recv_sem=head_recv.at[j - 1, index, low],
                    device_id={"head": head_peer[j]},
                    device_id_type=MESH,
                )
                copy.start()
                head_copies[index, j, low] = copy

    def send_sums(low, turn):
        for index in range(GROUP)[::-1]:
            mixed = partial[index, my_head * share + turn].astype(jnp.float32)
            for j in range(1, n_head):
                head_copies[index, j, low].wait_recv()
                mixed += arrived[j - 1, index, turn].astype(jnp.float32)
            target = summed if index else shared
            target[index, turn] = mixed.astype(jnp.bfloat16)
            if index:
                copy = pltpu.make_async_remote_copy(
                    src_ref=summed.at[index, turn],
                    dst_ref=shared.at[index, turn],
                    send_sem=out_send.at[index, low],
                    recv_sem=out_recv.at[index, low],
                    device_id={"ctx": member[index]},
                    device_id_type=MESH,
                )
                copy.start()
                out_copies.append(copy)

    late = set(held[len(order)])
    everything = [r for stage in held for r in stage]
    for low in range(share):
        turn = differing_bits(lax.rem(my_turn, share), low, low_bits)
        wanted_now = [r for r in everything if (r // GROUP) % share == low]
        for r in wanted_now:
            if r in late:
                for piece in range(PIECES):
                    wait_w(piece, r)
            if r != wanted_now[-1]:
                project(r)
        send_partials(low, turn, wanted_now[-1])
        send_sums(low, turn)
    for copy in out_copies:
        copy.wait_recv()

    pair = max(1, 128 // w_width)
    for first in range(0, share * GROUP, pair):
        parts = []
        for slot in range(first, first + pair):
            index = differing_bits(lax.rem(me, GROUP), slot % GROUP, (1, 2))
            parts.append(shared[index, slot // GROUP])
        whole = parts[0] if pair == 1 else jnp.concatenate(parts, axis=1)
        out_ref[:, pl.ds(first * w_width, pair * w_width)] = whole

    sent = open_sends + mark_copies + out_copies
    for copies in (kv_copies, att_copies, head_copies):
        sent.extend(copies.values())
    for copy in sent:
        copy.wait_send()


def on_device(n_ctx, n_head, queries, keys, values, pool_weight, out_weight, pattern):
    tok_rows, col_width = queries.shape
    heads = col_width // HEAD_DIMENSION
    depth, w_width = out_weight.shape
    land = pool_weight.shape[0]
    levels = n_ctx.bit_length() - 1
    turns = n_ctx // GROUP
    share = turns // n_head
    bf16 = jnp.bfloat16
    in_vmem = pl.BlockSpec(memory_space=pltpu.VMEM)
    in_place = pl.BlockSpec(memory_space=pl.ANY)
    return pl.pallas_call(
        functools.partial(layer_kernel, n_ctx, n_head),
        out_shape=jax.ShapeDtypeStruct((tok_rows, share * GROUP * w_width), bf16),
        in_specs=[in_vmem, in_place, in_place, in_vmem, in_place]
        + [pl.BlockSpec(memory_space=pltpu.SMEM)],
        out_specs=in_vmem,
        scratch_shapes=[pltpu.VMEM((tok_rows, col_width), bf16)] * (2 * levels + 2)
        + [
            pltpu.VMEM((turns, depth, w_width), bf16),
            pltpu.VMEM((n_ctx, 2 * land, col_width), bf16),
            pltpu.VMEM((heads, tok_rows, HEAD_DIMENSION), jnp.float32),
            pltpu.VMEM((heads, tok_rows, 1), jnp.float32),
            pltpu.VMEM((heads, tok_rows, 1), jnp.float32),
            pltpu.VMEM((GROUP, tok_rows, col_width), bf16),
            pltpu.VMEM((GROUP, turns, tok_rows, w_width), bf16),
            pltpu.VMEM((n_head - 1, GROUP, share, tok_rows, w_width), bf16),
            pltpu.VMEM((GROUP, share, tok_rows, w_width), bf16),
            pltpu.VMEM((GROUP, share, tok_rows, w_width), bf16),
            pltpu.SemaphoreType.DMA((levels, 2)),
            pltpu.SemaphoreType.DMA((levels, 2)),
            pltpu.SemaphoreType.DMA((PIECES, turns, levels)),
            pltpu.SemaphoreType.DMA((PIECES, turns)),
            pltpu.SemaphoreType.DMA((levels,)),
            pltpu.SemaphoreType.DMA((levels,)),
            pltpu.SemaphoreType.DMA((GROUP, 2)),
            pltpu.SemaphoreType.DMA((GROUP, 2)),
            pltpu.SemaphoreType.DMA((n_head - 1, GROUP, share)),
            pltpu.SemaphoreType.DMA((n_head - 1, GROUP, share)),
            pltpu.SemaphoreType.DMA((GROUP, share)),
            pltpu.SemaphoreType.DMA((GROUP, share)),
            pltpu.SemaphoreType.DMA((3,)),
        ],
        compiler_params=pltpu.CompilerParams(
            collective_id=0, has_side_effects=True, vmem_limit_bytes=56 * 1024 * 1024
        ),
    )(queries, keys, values, pool_weight, out_weight, pattern)


def solution(mesh):
    in_specs = (
        P("ctx", "head"),
        P("ctx", "head"),
        P("ctx", "head"),
        P("ctx", None),
        P("head", "ctx"),
        P(),
    )
    out_specs = P("ctx", "head")
    body = functools.partial(on_device, mesh.shape["ctx"], mesh.shape["head"])
    return jax.shard_map(
        body, mesh=mesh, in_specs=in_specs, out_specs=out_specs, check_vma=False
    )
```
